256 devices in a mesh: wide: 16 (over z, x_lo), narrow: 16 (over x_hi, y, core).
Axes of the slice: x: 4 (x_hi: 2, x_lo: 2; x = x_hi * 2 + x_lo), y: 4, z: 8, core: 2. Of those that a mesh axis runs over, the one named last changes fastest.
Arguments:
- panel: float32 [32, 4194304], P(None, ('wide', 'narrow'))
- signs: int32 [4194304], P(('wide', 'narrow')), may hold values from -1 to 1, as said below
- sample_rows: int32 [262144], P(('wide', 'narrow')), may hold values from 0 to 16383, as said below
- counts: int32 [256], P(('wide', 'narrow')), may hold values from 256 to 1024, as said below
Outputs:
- mixed: float32 [32, 4194304], P(None, ('wide', 'narrow'))
- gram: float32 [32, 32], replicated
The draws below stay inside these ranges and needn't reach their ends.
Inputs may be any that keep to these rules, and one draw needn't show every extreme that they name: `sample_rows`: within each block's 1024 slots the indices are distinct and increasing, each below 16384. `counts`: some block has all 1024 slots live. `signs`: each entry is +1 or -1.
All inputs are finite; a program needn't handle non-finite values.
Results may differ from the reference program's by a relative error of at most 0.000098.
Values sent between devices are 32-bit elements; how exact they have to be, the bound alone decides.
No kernel may reach another device: no remote copies, remote signals or barrier semaphores. Data moves between devices by JAX's collectives and lax.ppermute only.
A program may use at most 64 MiB of HBM per device.

```python
import math
import jax
import jax.numpy as jnp
from jax import lax

PANEL = 32
LOW = 32
HIGH = 128
SLABS = 4
SAMPLES = 1024
ROWS = 16384
BLOCKS = 256
N_WIDE = 16
N_NARROW = 16


def draw_panel(key, part):
    key = jax.random.fold_in(key, 4)
    first, second, third = jax.random.split(key, 3)
    total = BLOCKS * ROWS
    base = jax.random.normal(first, (PANEL, total), jnp.float32)
    row_scale = jnp.exp(jax.random.uniform(second, (1, total), jnp.float32, 0.0, math.log(10.0)))
    col_scale = jnp.exp(jax.random.uniform(third, (PANEL, 1), jnp.float32, 0.0, math.log(10.0)))
    return (base * row_scale * col_scale * 0.1).astype(jnp.float32)


def draw_signs(key, part):
    key = jax.random.fold_in(key, 3)
    return (2 * jax.random.randint(key, (BLOCKS * ROWS,), 0, 2) - 1).astype(jnp.int32)


def draw_sample_rows(key, part):
    key = jax.random.fold_in(key, 1)
    keys = jax.random.split(key, BLOCKS)

    def one_block(sub):
        return jnp.sort(jax.random.permutation(sub, ROWS)[:SAMPLES])
    return jax.vmap(one_block)(keys).reshape(-1).astype(jnp.int32)


def draw_counts(key, part):
    key = jax.random.fold_in(key, 2)
    least = SAMPLES // 4
    steps = jnp.arange(BLOCKS, dtype=jnp.int32)
    base = least + (SAMPLES - least) * steps // max(BLOCKS - 1, 1)
    jitter = jax.random.randint(key, (BLOCKS,), -(SAMPLES // 8), SAMPLES // 8 + 1)
    values = jnp.clip(base + jitter, least, SAMPLES)
    return values.at[BLOCKS - 1].set(SAMPLES).astype(jnp.int32)


def setup_inputs(seed: int = 0) -> dict:
    splits = jax.random.split(jax.random.key(seed), 5)
    return {
        "panel": draw_panel(jax.random.fold_in(splits[4], 71), 0),
        "signs": draw_signs(jax.random.fold_in(splits[4], 71), 0),
        "sample_rows": draw_sample_rows(jax.random.fold_in(splits[4], 71), 0),
        "counts": draw_counts(jax.random.fold_in(splits[4], 71), 0),
    }


def table(n):
    idx = jnp.arange(n)
    both = jnp.bitwise_and(idx[:, None], idx[None, :])
    total = jnp.zeros((n, n), jnp.int32)
    for bit in range(max(n.bit_length(), 1)):
        total = total + jnp.bitwise_and(jnp.right_shift(both, bit), 1)
    return (1 - 2 * jnp.bitwise_and(total, 1)).astype(jnp.float32)

def reference(panel, signs, sample_rows, counts):
    blocks = N_WIDE * N_NARROW
    width = panel.shape[0]
    signed = panel * signs.astype(jnp.float32)[None, :]
    work = signed.reshape(width, blocks * SLABS, LOW, HIGH)
    work = jnp.einsum('pslh,hk->pslk', work, table(HIGH), precision=lax.Precision.HIGHEST)
    work = jnp.einsum('pslk,lm->psmk', work, table(LOW), precision=lax.Precision.HIGHEST)
    work = work.reshape(width, blocks, ROWS)
    work = jnp.einsum('pdr,de->per', work, table(blocks), precision=lax.Precision.HIGHEST)
    mixed = (work * (1.0 / math.sqrt(LOW * HIGH * blocks))).reshape(width, blocks * ROWS)
    starts = (jnp.arange(blocks, dtype=jnp.int32) * ROWS)[:, None]
    where = (sample_rows.reshape(blocks, SAMPLES) + starts).reshape(-1).astype(jnp.int32)
    live = (jnp.arange(SAMPLES, dtype=jnp.int32)[None, :] < counts[:, None]).reshape(-1)
    picked = mixed[:, where] * live.astype(jnp.float32)[None, :]
    outer = jnp.einsum('pk,qk->pq', picked, picked, precision=lax.Precision.HIGHEST)
    gram = outer / jnp.sum(counts.astype(jnp.float32))
    return (mixed, gram)
```

```python
import math

import jax
import jax.numpy as jnp
from jax import lax
from jax.experimental import pallas as pl
from jax.experimental.pallas import tpu as pltpu
from jax.sharding import PartitionSpec as P

LOW = 32
HIGH = 128
LANES = 128
HALF = 64
AXES = ("wide", "narrow")


def signs_of(i, j, n):
    v = jnp.bitwise_and(i, j)
    shift = 1
    while shift < n.bit_length():
        v = jnp.bitwise_xor(v, jnp.right_shift(v, shift))
        shift *= 2
    return (1 - 2 * jnp.bitwise_and(v, 1)).astype(jnp.float32)


def split(x):
    hi = x.astype(jnp.bfloat16)
    lo = (x - hi.astype(jnp.float32)).astype(jnp.bfloat16)
    return hi, lo


def dot(a, b):
    return jnp.dot(a, b, preferred_element_type=jnp.float32)


def butterfly(vs):
    step = 1
    while step < len(vs):
        out = list(vs)
        for i in range(len(vs)):
            if not i & step:
                out[i] = vs[i] + vs[i | step]
                out[i | step] = vs[i] - vs[i | step]
        vs = out
        step *= 2
    return vs


def local_kernel(scale, counts_ref, panel_ref, signs_ref, rows_ref, out_ref, table_ref, even_ref, odd_ref, x_ref):
    s = pl.program_id(0)
    width = panel_ref.shape[0]
    lane = lax.broadcasted_iota(jnp.int32, (16, LANES), 1)

    @pl.when(s == 0)
    def _():
        i = lax.broadcasted_iota(jnp.int32, (HIGH, 2 * HIGH), 0)
        j = lax.broadcasted_iota(jnp.int32, (HIGH, 2 * HIGH), 1)
        j = jnp.where(j < HIGH, j, jnp.bitwise_and(j + HALF, HIGH - 1))
        table_ref[...] = (signs_of(i, j, HIGH) * scale).astype(jnp.bfloat16)
        rows = rows_ref[...]
        samples = rows.shape[1]
        slot = lax.broadcasted_iota(jnp.int32, (1, samples), 1)
        rows = jnp.where(slot < counts_ref[0], rows, -1)
        at = lax.broadcasted_iota(jnp.int32, (HIGH, samples), 0)
        tile = (jnp.right_shift(rows, 7) == at).astype(jnp.float32).astype(jnp.bfloat16)
        inner = (jnp.bitwise_and(rows, HIGH - 1) == at).astype(jnp.float32).astype(jnp.bfloat16)
        mask = lax.dot_general(tile, inner, (((1,), (1,)), ((), ())), preferred_element_type=jnp.float32)
        other = pltpu.roll(mask, HALF, 1)
        low = lax.broadcasted_iota(jnp.int32, (HIGH, LANES), 1) < HALF
        even_ref[...] = jnp.where(low, mask, other)
        odd_ref[...] = jnp.where(low, other, mask)

    for g in range(width // 8):
        vs = [
            panel_ref[8 * g : 8 * g + 8, LANES * a : LANES * (a + 1)]
            * signs_ref[:, LANES * a : LANES * (a + 1)].astype(jnp.float32)
            for a in range(LOW)
        ]
        for a, v in enumerate(butterfly(vs)):
            x_ref[width * a + 8 * g : width * a + 8 * g + 8, :] = v

    table = table_ref[...]
    per = 8
    for c in range(LOW // per):
        hi, lo = split(x_ref[width * per * c : width * per * (c + 1), :])
        z = dot(hi, table) + dot(lo, table)
        for k in range(per):
            a = per * c + k
            y = z[width * k : width * (k + 1), :LANES]
            r = z[width * k : width * (k + 1), LANES:]
            row = 34 * a
            out_ref[row : row + 16, :] = jnp.where(lane < HALF, y[:16], r[16:])
            out_ref[row + 16 : row + 17, :] = even_ref[pl.ds(LOW * s + a, 1), :]
            out_ref[row + 17 : row + 33, :] = jnp.where(lane < HALF, r[:16], y[16:])
            out_ref[row + 33 : row + 34, :] = odd_ref[pl.ds(LOW * s + a, 1), :]


def across_kernel(blocks, in_ref, out_ref, mask_ref):
    i = lax.broadcasted_iota(jnp.int32, (blocks, blocks), 0)
    j = lax.broadcasted_iota(jnp.int32, (blocks, blocks), 1)
    table = signs_of(i, j, blocks).astype(jnp.bfloat16)
    for k in range(0, 16, 2):
        x = jnp.concatenate(
            [in_ref[pl.ds(k, blocks, stride=17), :], in_ref[pl.ds(k + 1, blocks, stride=17), :]], axis=1
        )
        hi, lo = split(x)
        y = dot(table, hi) + dot(table, lo)
        out_ref[pl.ds(k, blocks, stride=16), :] = y[:, :LANES]
        out_ref[pl.ds(k + 1, blocks, stride=16), :] = y[:, LANES:]
    mask_ref[...] = in_ref[pl.ds(16, blocks, stride=17), :]


def gram_kernel(counts_ref, y_ref, mask_ref, out_ref):
    blocks = mask_ref.shape[0]
    low = lax.broadcasted_iota(jnp.int32, (16, LANES), 1) < HALF
    low1 = lax.broadcasted_iota(jnp.int32, (1, LANES), 1) < HALF
    pairs = 8

    def body(c, total):
        plain, masked = [], []
        for k in range(pairs):
            d = 2 * pairs * c + 2 * k
            first = y_ref[pl.ds(pl.multiple_of(d * 16, 32), 16), :]
            second = y_ref[pl.ds(pl.multiple_of(d * 16, 32) + 16, 16), :]
            both = jnp.concatenate(
                [
                    jnp.where(low, first, pltpu.roll(second, HALF, 1)),
                    jnp.where(low, pltpu.roll(first, HALF, 1), second),
                ],
                axis=0,
            )
            m = jnp.where(low1, mask_ref[pl.ds(d, 1), :], mask_ref[pl.ds(d + 1, 1), :])
            plain.append(both)
            masked.append(both * m)
        a_hi, a_lo = split(jnp.concatenate(masked, axis=1))
        b_hi, b_lo = split(jnp.concatenate(plain, axis=1))
        nt = (((1,), (1,)), ((), ()))
        for a, b in ((a_hi, b_hi), (a_hi, b_lo), (a_lo, b_hi)):
            total = total + lax.dot_general(a, b, nt, preferred_element_type=jnp.float32)
        return total

    total = lax.fori_loop(0, blocks // (2 * pairs), body, jnp.zeros((32, 32), jnp.float32))
    out_ref[:32, :] = total
    out_ref[32:, :] = jnp.full((8, 32), counts_ref[0].astype(jnp.float32))


def unpack_kernel(in_ref, out_ref):
    low = lax.broadcasted_iota(jnp.int32, (16, LANES), 1) < HALF
    for t in range(out_ref.shape[1] // LANES):
        even = in_ref[32 * t : 32 * t + 16, :]
        odd = in_ref[32 * t + 16 : 32 * t + 32, :]
        out_ref[:16, LANES * t : LANES * (t + 1)] = jnp.where(low, even, pltpu.roll(odd, HALF, 1))
        out_ref[16:, LANES * t : LANES * (t + 1)] = jnp.where(low, pltpu.roll(even, HALF, 1), odd)


def everywhere_sum(x):
    for axis, bits in (("narrow", (1, 2, 4, 8)), ("wide", (1, 2, 4, 8))):
        for bit in bits:
            x = x + lax.ppermute(x, axis, [(i, i ^ bit) for i in range(lax.axis_size(axis))])
    return x


SMEM = pl.BlockSpec(memory_space=pltpu.SMEM)


def shards(panel, signs, sample_rows, counts):
    width, length = panel.shape
    slab = LOW * HIGH
    slabs = length // slab
    blocks = lax.axis_size("wide") * lax.axis_size("narrow")
    samples = sample_rows.shape[0]
    scale = 1.0 / math.sqrt(slab * blocks)
    f32 = jnp.float32

    sent = pl.pallas_call(
        lambda *refs: local_kernel(scale, *refs),
        grid=(slabs,),
        in_specs=[
            SMEM,
            pl.BlockSpec((width, slab), lambda s: (0, s)),
            pl.BlockSpec((1, slab), lambda s: (0, s)),
            pl.BlockSpec((1, samples), lambda s: (0, 0)),
        ],
        out_specs=pl.BlockSpec((34 * LOW, LANES), lambda s: (s, 0)),
        out_shape=jax.ShapeDtypeStruct((34 * LOW * slabs, LANES), f32),
        scratch_shapes=[
            pltpu.VMEM((HIGH, 2 * HIGH), jnp.bfloat16),
            pltpu.VMEM((HIGH, LANES), f32),
            pltpu.VMEM((HIGH, LANES), f32),
            pltpu.VMEM((width * LOW, LANES), f32),
        ],
        compiler_params=pltpu.CompilerParams(vmem_limit_bytes=32 * 2**20),
    )(counts, panel, signs.reshape(1, length), sample_rows.reshape(1, samples))

    got = lax.all_to_all(sent.reshape(17 * blocks, 1, LANES), AXES, 0, 0, tiled=True).reshape(17 * blocks, LANES)

    mixed, mask = pl.pallas_call(
        lambda *refs: across_kernel(blocks, *refs),
        out_shape=(jax.ShapeDtypeStruct((16 * blocks, LANES), f32), jax.ShapeDtypeStruct((blocks, LANES), f32)),
        compiler_params=pltpu.CompilerParams(vmem_limit_bytes=32 * 2**20),
    )(got)

    back = lax.all_to_all(mixed, AXES, 0, 0, tiled=True)

    part = pl.pallas_call(
        gram_kernel,
        in_specs=[SMEM, pl.BlockSpec(memory_space=pltpu.VMEM), pl.BlockSpec(memory_space=pltpu.VMEM)],
        out_shape=jax.ShapeDtypeStruct((40, 32), f32),
        compiler_params=pltpu.CompilerParams(vmem_limit_bytes=32 * 2**20),
    )(counts, mixed, mask)
    total = everywhere_sum(part)
    gram = total[:32] / total[32, 0]

    out = pl.pallas_call(
        unpack_kernel,
        grid=(slabs,),
        in_specs=[pl.BlockSpec((32 * LOW, LANES), lambda s: (s, 0))],
        out_specs=pl.BlockSpec((width, slab), lambda s: (0, s)),
        out_shape=jax.ShapeDtypeStruct((width, length), f32),
        compiler_params=pltpu.CompilerParams(vmem_limit_bytes=32 * 2**20),
    )(back)
    return out, gram


def solution(mesh):
    placed = (P(None, AXES), P(AXES), P(AXES), P(AXES))
    return jax.shard_map(
        shards,
        mesh=mesh,
        in_specs=placed,
        out_specs=(P(None, AXES), P()),
        check_vma=False,
    )
```

```python
import math

import jax
import jax.numpy as jnp
from jax import lax
from jax.experimental import pallas as pl
from jax.experimental.pallas import tpu as pltpu
from jax.sharding import PartitionSpec as P

LOW = 32
HIGH = 128
LANES = 128
HALF = 64
AXES = ("wide", "narrow")


def signs_of(i, j, n):
    v = jnp.bitwise_and(i, j)
    shift = 1
    while shift < n.bit_length():
        v = jnp.bitwise_xor(v, jnp.right_shift(v, shift))
        shift *= 2
    return (1 - 2 * jnp.bitwise_and(v, 1)).astype(jnp.float32)


def split(x):
    hi = x.astype(jnp.bfloat16)
    lo = (x - hi.astype(jnp.float32)).astype(jnp.bfloat16)
    return hi, lo


def dot(a, b):
    return jnp.dot(a, b, preferred_element_type=jnp.float32)


def butterfly(vs):
    step = 1
    while step < len(vs):
        out = list(vs)
        for i in range(len(vs)):
            if not i & step:
                out[i] = vs[i] + vs[i | step]
                out[i | step] = vs[i] - vs[i | step]
        vs = out
        step *= 2
    return vs


def local_kernel(
    scale, counts_ref, panel_hbm, signs_hbm, rows_hbm, out_hbm,
    panel_ref, signs_ref, rows_ref, table_ref, even_ref, odd_ref, x_ref, out_ref, sems, out_sems,
):
    slabs, width, slab = panel_ref.shape
    small = [
        pltpu.make_async_copy(rows_hbm, rows_ref, sems.at[slabs]),
        pltpu.make_async_copy(signs_hbm, signs_ref, sems.at[slabs + 1]),
    ]
    big = [
        pltpu.make_async_copy(panel_hbm.at[:, slab * s : slab * (s + 1)], panel_ref.at[s], sems.at[s])
        for s in range(slabs)
    ]
    for copy in small + big:
        copy.start()
    i = lax.broadcasted_iota(jnp.int32, (2 * HIGH, 2 * HIGH), 0)
    j = lax.broadcasted_iota(jnp.int32, (2 * HIGH, 2 * HIGH), 1)
    i = jnp.bitwise_and(i, HIGH - 1)
    j = jnp.where(j < HIGH, j, jnp.bitwise_and(j + HALF, HIGH - 1))
    table_ref[...] = (signs_of(i, j, HIGH) * scale).astype(jnp.bfloat16)
    small[0].wait()
    rows = rows_ref[...]
    samples = rows.shape[1]
    slot = lax.broadcasted_iota(jnp.int32, (1, samples), 1)
    rows = jnp.where(slot < counts_ref[0], rows, -1)
    at = lax.broadcasted_iota(jnp.int32, (HIGH, samples), 0)
    tile = (jnp.right_shift(rows, 7) == at).astype(jnp.float32).astype(jnp.bfloat16)
    inner = (jnp.bitwise_and(rows, HIGH - 1) == at).astype(jnp.float32).astype(jnp.bfloat16)
    mask = lax.dot_general(tile, inner, (((1,), (1,)), ((), ())), preferred_element_type=jnp.float32)
    other = pltpu.roll(mask, HALF, 1)
    low = lax.broadcasted_iota(jnp.int32, (HIGH, LANES), 1) < HALF
    even_ref[...] = jnp.where(low, mask, other)
    odd_ref[...] = jnp.where(low, other, mask)
    small[1].wait()
    table = table_ref[...]
    low = lax.broadcasted_iota(jnp.int32, (16, LANES), 1) < HALF
    per = 8
    outs = []
    for s in range(slabs):
        big[s].wait()
        for g in range(width // 8):
            vs = [
                panel_ref[s, 8 * g : 8 * g + 8, LANES * a : LANES * (a + 1)]
                * signs_ref[:, slab * s + LANES * a : slab * s + LANES * (a + 1)].astype(jnp.float32)
                for a in range(LOW)
            ]
            for a, v in enumerate(butterfly(vs)):
                x_ref[s % 2, width * a + 8 * g : width * a + 8 * g + 8, :] = v
        for c in range(LOW // per):
            hi, lo = split(x_ref[s % 2, width * per * c : width * per * (c + 1), :])
            z = dot(jnp.concatenate([hi, lo], axis=1), table)
            for k in range(per):
                t = LOW * s + per * c + k
                y = z[width * k : width * (k + 1), :LANES]
                r = z[width * k : width * (k + 1), LANES:]
                row = 34 * t
                out_ref[row : row + 16, :] = jnp.where(low, y[:16], r[16:])
                out_ref[row + 16 : row + 17, :] = even_ref[t : t + 1, :]
                out_ref[row + 17 : row + 33, :] = jnp.where(low, r[:16], y[16:])
                out_ref[row + 33 : row + 34, :] = odd_ref[t : t + 1, :]
        rows = pl.ds(34 * LOW * s, 34 * LOW)
        outs.append(pltpu.make_async_copy(out_ref.at[rows, :], out_hbm.at[rows, :], out_sems.at[s]))
        outs[-1].start()
    for copy in outs:
        copy.wait()


def across_kernel(blocks, in_ref, out_hbm, mask_hbm, keep_ref, mask_ref, sems):
    i = lax.broadcasted_iota(jnp.int32, (blocks, blocks), 0)
    j = lax.broadcasted_iota(jnp.int32, (blocks, blocks), 1)
    table = signs_of(i, j, blocks).astype(jnp.bfloat16)
    tiles = keep_ref.reshape(blocks, 16, LANES)
    mask_ref[...] = in_ref[pl.ds(16, blocks, stride=17), :]
    copies = [pltpu.make_async_copy(mask_ref, mask_hbm, sems.at[2])]
    copies[0].start()
    for part in range(2):
        for k in range(8 * part, 8 * part + 8, 2):
            x = jnp.concatenate(
                [in_ref[pl.ds(k, blocks, stride=17), :], in_ref[pl.ds(k + 1, blocks, stride=17), :]], axis=1
            )
            hi, lo = split(x)
            y = dot(table, hi) + dot(table, lo)
            keep_ref[pl.ds(k, blocks, stride=16), :] = y[:, :LANES]
            keep_ref[pl.ds(k + 1, blocks, stride=16), :] = y[:, LANES:]
        rows = pl.ds(8 * part, 8)
        copies.append(pltpu.make_async_copy(tiles.at[:, rows, :], out_hbm.at[:, rows, :], sems.at[part]))
        copies[-1].start()
    for copy in copies:
        copy.wait()


def gram_kernel(counts_ref, y_ref, mask_ref, out_ref):
    blocks = mask_ref.shape[0]
    low = lax.broadcasted_iota(jnp.int32, (16, LANES), 1) < HALF
    low1 = lax.broadcasted_iota(jnp.int32, (1, LANES), 1) < HALF
    pairs = 8

    @pl.when(pl.program_id(0) == 0)
    def _():
        out_ref[:32, :] = jnp.zeros((32, 32), jnp.float32)
        out_ref[32:, :] = jnp.full((8, 32), counts_ref[0].astype(jnp.float32))

    total = out_ref[:32, :]
    for c in range(blocks // (2 * pairs)):
        plain, masked = [], []
        for k in range(pairs):
            d = 2 * pairs * c + 2 * k
            first = y_ref[d]
            second = y_ref[d + 1]
            both = jnp.concatenate(
                [
                    jnp.where(low, first, pltpu.roll(second, HALF, 1)),
                    jnp.where(low, pltpu.roll(first, HALF, 1), second),
                ],
                axis=0,
            )
            m = jnp.where(low1, mask_ref[d : d + 1, :], mask_ref[d + 1 : d + 2, :])
            plain.append(both)
            masked.append(both * m)
        a_hi, a_lo = split(jnp.concatenate(masked, axis=1))
        b_hi, b_lo = split(jnp.concatenate(plain, axis=1))
        nt = (((1,), (1,)), ((), ()))
        for a, b in ((a_hi, b_hi), (a_hi, b_lo), (a_lo, b_hi)):
            total = total + lax.dot_general(a, b, nt, preferred_element_type=jnp.float32)
    out_ref[:32, :] = total


def unpack_kernel(in_ref, out_ref):
    low = lax.broadcasted_iota(jnp.int32, (16, LANES), 1) < HALF
    for t in range(out_ref.shape[1] // LANES):
        even = in_ref[32 * t : 32 * t + 16, :]
        odd = in_ref[32 * t + 16 : 32 * t + 32, :]
        out_ref[:16, LANES * t : LANES * (t + 1)] = jnp.where(low, even, pltpu.roll(odd, HALF, 1))
        out_ref[16:, LANES * t : LANES * (t + 1)] = jnp.where(low, pltpu.roll(even, HALF, 1), odd)


def send(x, move):
    wide, narrow = lax.axis_size("wide"), lax.axis_size("narrow")
    pairs = []
    for w in range(wide):
        for n in range(narrow):
            to = move(w, n)
            if to is not None:
                pairs.append((w * narrow + n, to[0] * narrow + to[1]))
    return lax.ppermute(x, AXES, pairs)


def half_sum(x):
    x = x + send(x, lambda w, n: (w, n ^ 1))
    x = x + send(x, lambda w, n: (w, n ^ 2)) + send(x, lambda w, n: (w, n ^ 4)) + send(x, lambda w, n: (w, n ^ 6))
    x = x + send(x, lambda w, n: (w ^ 1, n)) + send(x, lambda w, n: (w, n ^ 8)) + send(x, lambda w, n: (w ^ 1, n ^ 8))
    far = lax.axis_size("wide") // 2
    own = jnp.where(jnp.bitwise_and(lax.axis_index("narrow"), 1) == 0, x, 0.0)
    half = far // 2
    for step in range(half):
        own = own + send(
            x,
            lambda w, n, step=step: (w ^ (2 * (step + half * (n & 1))), n) if step + (n & 1) else None,
        )
    return own


SMEM = pl.BlockSpec(memory_space=pltpu.SMEM)
VMEM = pl.BlockSpec(memory_space=pltpu.VMEM)
HBM = pl.BlockSpec(memory_space=pltpu.HBM)


def shards(panel, signs, sample_rows, counts):
    width, length = panel.shape
    slab = LOW * HIGH
    slabs = length // slab
    blocks = lax.axis_size("wide") * lax.axis_size("narrow")
    samples = sample_rows.shape[0]
    scale = 1.0 / math.sqrt(slab * blocks)
    f32 = jnp.float32

    sent = pl.pallas_call(
        lambda *refs: local_kernel(scale, *refs),
        in_specs=[SMEM, HBM, HBM, HBM],
        out_specs=HBM,
        out_shape=jax.ShapeDtypeStruct((17 * blocks, LANES), f32),
        scratch_shapes=[
            pltpu.VMEM((slabs, width, slab), f32),
            pltpu.VMEM((1, length), jnp.int32),
            pltpu.VMEM((1, samples), jnp.int32),
            pltpu.VMEM((2 * HIGH, 2 * HIGH), jnp.bfloat16),
            pltpu.VMEM((HIGH, LANES), f32),
            pltpu.VMEM((HIGH, LANES), f32),
            pltpu.VMEM((2, width * LOW, LANES), f32),
            pltpu.VMEM((17 * blocks, LANES), f32),
            pltpu.SemaphoreType.DMA((slabs + 2,)),
            pltpu.SemaphoreType.DMA((slabs,)),
        ],
        compiler_params=pltpu.CompilerParams(vmem_limit_bytes=60 * 2**20),
    )(counts, panel, signs.reshape(1, length), sample_rows.reshape(1, samples))

    got = lax.all_to_all(sent.reshape(17 * blocks, 1, LANES), AXES, 0, 0, tiled=True).reshape(17 * blocks, LANES)

    mixed, mask = pl.pallas_call(
        lambda *refs: across_kernel(blocks, *refs),
        in_specs=[VMEM],
        out_specs=(HBM, HBM),
        out_shape=(pltpu.HBM((blocks, 16, LANES), f32), pltpu.HBM((blocks, LANES), f32)),
        scratch_shapes=[
            pltpu.VMEM((16 * blocks, LANES), f32),
            pltpu.VMEM((blocks, LANES), f32),
            pltpu.SemaphoreType.DMA((3,)),
        ],
        compiler_params=pltpu.CompilerParams(vmem_limit_bytes=32 * 2**20),
    )(got)

    back = lax.all_to_all(mixed, AXES, 0, 0, tiled=True).reshape(16 * blocks, LANES)

    steps = 8
    part = pl.pallas_call(
        gram_kernel,
        grid=(steps,),
        in_specs=[
            SMEM,
            pl.BlockSpec((blocks // steps, 16, LANES), lambda s: (s, 0, 0)),
            pl.BlockSpec((blocks // steps, LANES), lambda s: (s, 0)),
        ],
        out_specs=pl.BlockSpec((40, 32), lambda s: (0, 0)),
        out_shape=jax.ShapeDtypeStruct((40, 32), f32),
        compiler_params=pltpu.CompilerParams(vmem_limit_bytes=60 * 2**20),
    )(counts, mixed, mask)
    total, back = lax.optimization_barrier((half_sum(part), back))
    total = total + send(total, lambda w, n: (w, n ^ 1))
    gram = total[:32] / total[32:33]

    out = pl.pallas_call(
        unpack_kernel,
        grid=(slabs,),
        in_specs=[pl.BlockSpec((32 * LOW, LANES), lambda s: (s, 0))],
        out_specs=pl.BlockSpec((width, slab), lambda s: (0, s)),
        out_shape=jax.ShapeDtypeStruct((width, length), f32),
        compiler_params=pltpu.CompilerParams(vmem_limit_bytes=32 * 2**20),
    )(back)
    return out, gram


def solution(mesh):
    placed = (P(None, AXES), P(AXES), P(AXES), P(AXES))
    return jax.shard_map(
        shards,
        mesh=mesh,
        in_specs=placed,
        out_specs=(P(None, AXES), P()),
        check_vma=False,
    )
```

```python
import math

import jax
import jax.numpy as jnp
from jax import lax
from jax.experimental import pallas as pl
from jax.experimental.pallas import tpu as pltpu
from jax.sharding import Mesh
from jax.sharding import PartitionSpec as P

LOW = 32
HIGH = 128
LANES = 128
CHIP = ("wide", "high")
AXES = ("wide", "high", "core")
SMEM = pl.BlockSpec(memory_space=pltpu.SMEM)
VMEM = pl.BlockSpec(memory_space=pltpu.VMEM)
HBM = pl.BlockSpec(memory_space=pltpu.HBM)
PARAMS = pltpu.CompilerParams(vmem_limit_bytes=32 * 2**20)


def signs_of(i, j, n):
    v = jnp.bitwise_and(i, j)
    shift = 1
    while shift < n.bit_length():
        v = jnp.bitwise_xor(v, jnp.right_shift(v, shift))
        shift *= 2
    return (1 - 2 * jnp.bitwise_and(v, 1)).astype(jnp.float32)


def split(x):
    hi = x.astype(jnp.bfloat16)
    lo = (x - hi.astype(jnp.float32)).astype(jnp.bfloat16)
    return hi, lo


def dot(a, b):
    return jnp.dot(a, b, preferred_element_type=jnp.float32)


def butterfly(vs):
    step = 1
    while step < len(vs):
        out = list(vs)
        for i in range(len(vs)):
            if not i & step:
                out[i] = vs[i] + vs[i | step]
                out[i | step] = vs[i] - vs[i | step]
        vs = out
        step *= 2
    return vs


def prepare_kernel(counts_ref, rows_ref, panel_ref, signs_ref, mask_ref, own_ref):
    rows = rows_ref[...]
    samples = rows.shape[1]
    slot = lax.broadcasted_iota(jnp.int32, (1, samples), 1)
    rows = jnp.where(slot < counts_ref[0], rows, -1)
    at = lax.broadcasted_iota(jnp.int32, (HIGH, samples), 0)
    tile = (jnp.right_shift(rows, 7) == at).astype(jnp.float32).astype(jnp.bfloat16)
    inner = (jnp.bitwise_and(rows, HIGH - 1) == at).astype(jnp.float32).astype(jnp.bfloat16)
    mask_ref[...] = lax.dot_general(tile, inner, (((1,), (1,)), ((), ())), preferred_element_type=jnp.float32)
    own_sign = 1 - 2 * lax.axis_index("core")
    own_ref[...] = panel_ref[...] * (signs_ref[...] * own_sign).astype(jnp.float32)


def local_kernel(scale, own_ref, other_ref, other_signs_ref, mask_ref, out_ref, x_ref):
    width, length = own_ref.shape
    slab = LOW * HIGH
    i = lax.broadcasted_iota(jnp.int32, (2 * HIGH, HIGH), 0)
    j = lax.broadcasted_iota(jnp.int32, (2 * HIGH, HIGH), 1)
    table = (signs_of(jnp.bitwise_and(i, HIGH - 1), j, HIGH) * scale).astype(jnp.bfloat16)
    per = 8
    for s in range(length // slab):
        for g in range(width // 8):
            vs = []
            for a in range(LOW):
                cols = slice(slab * s + LANES * a, slab * s + LANES * (a + 1))
                rows = slice(8 * g, 8 * g + 8)
                vs.append(own_ref[rows, cols] + other_ref[rows, cols] * other_signs_ref[:, cols].astype(jnp.float32))
            for a, v in enumerate(butterfly(vs)):
                x_ref[s % 2, width * a + 8 * g : width * a + 8 * g + 8, :] = v
        for c in range(LOW // per):
            hi, lo = split(x_ref[s % 2, width * per * c : width * per * (c + 1), :])
            z = dot(jnp.concatenate([hi, lo], axis=1), table)
            for k in range(per):
                t = LOW * s + per * c + k
                row = (width + 1) * t
                out_ref[row : row + width, :] = z[width * k : width * (k + 1), :]
                out_ref[row + width : row + width + 1, :] = mask_ref[t : t + 1, :]


def across_kernel(chips, width, in_ref, out_hbm, mask_hbm, keep_ref, mask_ref, sems):
    i = lax.broadcasted_iota(jnp.int32, (chips, 2 * chips), 0)
    j = lax.broadcasted_iota(jnp.int32, (chips, 2 * chips), 1)
    table = signs_of(i, jnp.where(j < chips, j, j - chips), chips).astype(jnp.bfloat16)
    mask_ref[...] = in_ref[pl.ds(width, chips, stride=width + 1), :]
    copies = [pltpu.make_async_copy(mask_ref, mask_hbm, sems.at[width // 8])]
    copies[0].start()
    tiles = keep_ref.reshape(chips, width, LANES)
    for part in range(width // 8):
        for k in range(8 * part, 8 * part + 8, 2):
            x = jnp.concatenate(
                [in_ref[pl.ds(k + n, chips, stride=width + 1), :] for n in range(2)], axis=1
            )
            y = dot(table, jnp.concatenate(split(x), axis=0))
            for n in range(2):
                keep_ref[pl.ds(k + n, chips, stride=width), :] = y[:, LANES * n : LANES * (n + 1)]
        rows = pl.ds(8 * part, 8)
        copies.append(pltpu.make_async_copy(tiles.at[:, rows, :], out_hbm.at[:, rows, :], sems.at[part]))
        copies[-1].start()
    for copy in copies:
        copy.wait()


def gram_kernel(counts_ref, y_ref, mask_ref, out_ref):
    blocks, width, _ = y_ref.shape

    @pl.when(pl.program_id(0) == 0)
    def _():
        out_ref[:width, :] = jnp.zeros((width, width), jnp.float32)
        out_ref[width:, :] = jnp.full((8, width), counts_ref[0].astype(jnp.float32))

    total = out_ref[:width, :]
    per = 8
    for c in range(0, blocks, per):
        plain = jnp.concatenate([y_ref[d] for d in range(c, c + per)], axis=1)
        masked = jnp.concatenate([y_ref[d] * mask_ref[d : d + 1, :] for d in range(c, c + per)], axis=1)
        a_hi, a_lo = split(masked)
        b_hi, b_lo = split(plain)
        nt = (((1,), (1,)), ((), ()))
        for a, b in ((a_hi, b_hi), (a_hi, b_lo), (a_lo, b_hi)):
            total = total + lax.dot_general(a, b, nt, preferred_element_type=jnp.float32)
    out_ref[:width, :] = total


def unpack_kernel(in_ref, out_ref):
    for t in range(in_ref.shape[0]):
        out_ref[:, LANES * t : LANES * (t + 1)] = in_ref[t]


def send(x, move):
    wide, high, core = (lax.axis_size(axis) for axis in AXES)
    pairs = []
    for w in range(wide):
        for h in range(high):
            for c in range(core):
                to = move(w, h, c)
                if to is not None:
                    pairs.append(((w * high + h) * core + c, (to[0] * high + to[1]) * core + to[2]))
    return lax.ppermute(x, AXES, pairs)


def half_sum(x):
    x = x + send(x, lambda w, h, c: (w, h, c ^ 1))
    x = x + sum(send(x, lambda w, h, c, n=n: (w, h ^ n, c)) for n in (1, 2, 3))
    x = x + sum(send(x, lambda w, h, c, n=n: (w ^ (n & 1), h ^ (2 * (n & 2)), c)) for n in (1, 2, 3))
    half = lax.axis_size("wide") // 4
    own = jnp.where(lax.axis_index("core") == 0, x, 0.0)
    for step in range(half):
        own = own + send(
            x,
            lambda w, h, c, step=step: (w ^ (2 * (step + half * c)), h, c) if step + c else None,
        )
    return own


def shards(panel, signs, sample_rows, counts):
    width, length = panel.shape
    slab = LOW * HIGH
    chips = lax.axis_size("wide") * lax.axis_size("high")
    samples = sample_rows.shape[0]
    scale = 1.0 / math.sqrt(slab * chips * lax.axis_size("core"))
    f32 = jnp.float32
    message = width + 1

    swap = [(0, 1), (1, 0)]
    other = lax.ppermute(panel, "core", swap)
    other_signs = lax.ppermute(signs, "core", swap)

    live, own = pl.pallas_call(
        prepare_kernel,
        in_specs=[SMEM, VMEM, VMEM, VMEM],
        out_shape=(jax.ShapeDtypeStruct((chips, LANES), f32), jax.ShapeDtypeStruct((width, length), f32)),
        compiler_params=PARAMS,
    )(counts, sample_rows.reshape(1, samples), panel, signs.reshape(1, length))

    sent = pl.pallas_call(
        lambda *refs: local_kernel(scale, *refs),
        out_shape=jax.ShapeDtypeStruct((message * chips, LANES), f32),
        scratch_shapes=[pltpu.VMEM((2, width * LOW, LANES), f32)],
        compiler_params=PARAMS,
    )(own, other, other_signs.reshape(1, length), live)

    got = lax.all_to_all(sent.reshape(message * chips, 1, LANES), CHIP, 0, 0, tiled=True)

    mixed, mask = pl.pallas_call(
        lambda *refs: across_kernel(chips, width, *refs),
        in_specs=[VMEM],
        out_specs=(HBM, HBM),
        out_shape=(pltpu.HBM((chips, width, LANES), f32), pltpu.HBM((chips, LANES), f32)),
        scratch_shapes=[
            pltpu.VMEM((width * chips, LANES), f32),
            pltpu.VMEM((chips, LANES), f32),
            pltpu.SemaphoreType.DMA((width // 8 + 1,)),
        ],
        compiler_params=PARAMS,
    )(got.reshape(message * chips, LANES))

    back = lax.all_to_all(mixed, CHIP, 0, 0, tiled=True)

    steps = 8
    part = pl.pallas_call(
        gram_kernel,
        grid=(steps,),
        in_specs=[
            SMEM,
            pl.BlockSpec((chips // steps, width, LANES), lambda s: (s, 0, 0)),
            pl.BlockSpec((chips // steps, LANES), lambda s: (s, 0)),
        ],
        out_specs=pl.BlockSpec((width + 8, width), lambda s: (0, 0)),
        out_shape=jax.ShapeDtypeStruct((width + 8, width), f32),
        compiler_params=pltpu.CompilerParams(vmem_limit_bytes=60 * 2**20),
    )(counts, mixed, mask)
    total = half_sum(part)
    total = total + send(total, lambda w, h, c: (w, h, c ^ 1))
    gram = total[:width] / total[width : width + 1]

    pieces = 4
    out = pl.pallas_call(
        unpack_kernel,
        grid=(pieces,),
        in_specs=[pl.BlockSpec((chips // pieces, width, LANES), lambda s: (s, 0, 0))],
        out_specs=pl.BlockSpec((width, length // pieces), lambda s: (0, s)),
        out_shape=jax.ShapeDtypeStruct((width, length), f32),
        compiler_params=PARAMS,
    )(back)
    return out, gram


def solution(mesh):
    wide, narrow = mesh.devices.shape
    mesh = Mesh(mesh.devices.reshape(wide, narrow // 2, 2), AXES)
    placed = (P(None, AXES), P(AXES), P(AXES), P(AXES))
    return jax.shard_map(
        shards,
        mesh=mesh,
        in_specs=placed,
        out_specs=(P(None, AXES), P()),
        check_vma=False,
    )
```

```python
import math

import jax
import jax.numpy as jnp
from jax import lax
from jax.experimental import pallas as pl
from jax.experimental.pallas import tpu as pltpu
from jax.sharding import Mesh
from jax.sharding import PartitionSpec as P

LOW = 32
HIGH = 128
LANES = 128
FAR = ((8, 6), (4, 5))
CHIP = ("wide", "high")
AXES = ("wide", "high", "core")
SMEM = pl.BlockSpec(memory_space=pltpu.SMEM)
VMEM = pl.BlockSpec(memory_space=pltpu.VMEM)
HBM = pl.BlockSpec(memory_space=pltpu.HBM)
PARAMS = pltpu.CompilerParams(vmem_limit_bytes=32 * 2**20)


def signs_of(i, j, n):
    v = jnp.bitwise_and(i, j)
    shift = 1
    while shift < n.bit_length():
        v = jnp.bitwise_xor(v, jnp.right_shift(v, shift))
        shift *= 2
    return (1 - 2 * jnp.bitwise_and(v, 1)).astype(jnp.float32)


def split(x):
    hi = x.astype(jnp.bfloat16)
    lo = (x - hi.astype(jnp.float32)).astype(jnp.bfloat16)
    return hi, lo


def dot(a, b):
    return jnp.dot(a, b, preferred_element_type=jnp.float32)


def butterfly(vs):
    step = 1
    while step < len(vs):
        out = list(vs)
        for i in range(len(vs)):
            if not i & step:
                out[i] = vs[i] + vs[i | step]
                out[i | step] = vs[i] - vs[i | step]
        vs = out
        step *= 2
    return vs


def prepare_kernel(counts_ref, rows_ref, panel_ref, signs_ref, mask_ref, own_ref):
    rows = rows_ref[...]
    samples = rows.shape[1]
    slot = lax.broadcasted_iota(jnp.int32, (1, samples), 1)
    rows = jnp.where(slot < counts_ref[0], rows, -1)
    at = lax.broadcasted_iota(jnp.int32, (HIGH, samples), 0)
    tile = (jnp.right_shift(rows, 7) == at).astype(jnp.float32).astype(jnp.bfloat16)
    inner = (jnp.bitwise_and(rows, HIGH - 1) == at).astype(jnp.float32).astype(jnp.bfloat16)
    mask_ref[...] = lax.dot_general(tile, inner, (((1,), (1,)), ((), ())), preferred_element_type=jnp.float32)
    own_sign = 1 - 2 * lax.axis_index("core")
    own_ref[...] = panel_ref[...] * (signs_ref[...] * own_sign).astype(jnp.float32)


def local_kernel(scale, own_ref, other_ref, other_signs_ref, mask_ref, out_ref, x_ref):
    width, length = own_ref.shape
    slab = LOW * HIGH
    i = lax.broadcasted_iota(jnp.int32, (2 * HIGH, HIGH), 0)
    j = lax.broadcasted_iota(jnp.int32, (2 * HIGH, HIGH), 1)
    table = (signs_of(jnp.bitwise_and(i, HIGH - 1), j, HIGH) * scale).astype(jnp.bfloat16)
    per = 8
    for s in range(length // slab):
        for g in range(width // 8):
            vs = []
            for a in range(LOW):
                cols = slice(slab * s + LANES * a, slab * s + LANES * (a + 1))
                rows = slice(8 * g, 8 * g + 8)
                vs.append(own_ref[rows, cols] + other_ref[rows, cols] * other_signs_ref[:, cols].astype(jnp.float32))
            for a, v in enumerate(butterfly(vs)):
                x_ref[s % 2, width * a + 8 * g : width * a + 8 * g + 8, :] = v
        for c in range(LOW // per):
            hi, lo = split(x_ref[s % 2, width * per * c : width * per * (c + 1), :])
            z = dot(jnp.concatenate([hi, lo], axis=1), table)
            for k in range(per):
                t = LOW * s + per * c + k
                row = (width + 1) * t
                out_ref[row : row + width, :] = z[width * k : width * (k + 1), :]
                out_ref[row + width : row + width + 1, :] = mask_ref[t : t + 1, :]


def across_kernel(chips, width, in_ref, out_hbm, mask_hbm, keep_ref, mask_ref, sems):
    i = lax.broadcasted_iota(jnp.int32, (chips, 2 * chips), 0)
    j = lax.broadcasted_iota(jnp.int32, (chips, 2 * chips), 1)
    table = signs_of(i, jnp.where(j < chips, j, j - chips), chips).astype(jnp.bfloat16)
    mask_ref[...] = in_ref[pl.ds(width, chips, stride=width + 1), :]
    copies = [pltpu.make_async_copy(mask_ref, mask_hbm, sems.at[width // 8])]
    copies[0].start()
    tiles = keep_ref.reshape(chips, width, LANES)
    for part in range(width // 8):
        for k in range(8 * part, 8 * part + 8, 2):
            x = jnp.concatenate(
                [in_ref[pl.ds(k + n, chips, stride=width + 1), :] for n in range(2)], axis=1
            )
            y = dot(table, jnp.concatenate(split(x), axis=0))
            for n in range(2):
                keep_ref[pl.ds(k + n, chips, stride=width), :] = y[:, LANES * n : LANES * (n + 1)]
        rows = pl.ds(8 * part, 8)
        copies.append(pltpu.make_async_copy(tiles.at[:, rows, :], out_hbm.at[:, rows, :], sems.at[part]))
        copies[-1].start()
    for copy in copies:
        copy.wait()


def gram_kernel(counts_ref, y_ref, mask_ref, out_ref):
    blocks, width, _ = y_ref.shape

    @pl.when(pl.program_id(0) == 0)
    def _():
        out_ref[:width, :] = jnp.zeros((width, width), jnp.float32)
        out_ref[width:, :] = jnp.full((8, width), counts_ref[0].astype(jnp.float32))

    total = out_ref[:width, :]
    per = 8
    for c in range(0, blocks, per):
        plain = jnp.concatenate([y_ref[d] for d in range(c, c + per)], axis=1)
        masked = jnp.concatenate([y_ref[d] * mask_ref[d : d + 1, :] for d in range(c, c + per)], axis=1)
        a_hi, a_lo = split(masked)
        b_hi, b_lo = split(plain)
        nt = (((1,), (1,)), ((), ()))
        for a, b in ((a_hi, b_hi), (a_hi, b_lo), (a_lo, b_hi)):
            total = total + lax.dot_general(a, b, nt, preferred_element_type=jnp.float32)
    out_ref[:width, :] = total


def unpack_kernel(in_ref, out_ref):
    for t in range(in_ref.shape[0]):
        out_ref[:, LANES * t : LANES * (t + 1)] = in_ref[t]


def send(x, move):
    wide, high, core = (lax.axis_size(axis) for axis in AXES)
    pairs = []
    for w in range(wide):
        for h in range(high):
            for c in range(core):
                to = move(w, h, c)
                if to is not None:
                    pairs.append(((w * high + h) * core + c, (to[0] * high + to[1]) * core + to[2]))
    return lax.ppermute(x, AXES, pairs)


def paired_counts(counts):
    got, side = counts, 0
    for far_w, far_h in FAR:
        got = send(got, lambda w, h, c: (w ^ far_w, h ^ far_h, c) if c else None)
        side ^= far_w
    first = jnp.bitwise_and(lax.axis_index("wide"), side & -side) == 0
    return jnp.where(lax.axis_index("core") == 0, counts, jnp.where(first, counts + got, 0)), got


def half_sum(x):
    x = x + send(x, lambda w, h, c: (w, h, c ^ 1))
    x = x + sum(send(x, lambda w, h, c, n=n: (w, h ^ n, c)) for n in (1, 2, 3))
    x = x + sum(send(x, lambda w, h, c, n=n: (w ^ (n & 1), h ^ (2 * (n & 2)), c)) for n in (1, 2, 3))
    half = lax.axis_size("wide") // 4
    own = jnp.where(lax.axis_index("core") == 0, x, 0.0)
    for step in range(half):
        own = own + send(
            x,
            lambda w, h, c, step=step: (w ^ (2 * (step + half * c)), h, c) if step + c else None,
        )
    return own


def shards(panel, signs, sample_rows, counts):
    width, length = panel.shape
    slab = LOW * HIGH
    chips = lax.axis_size("wide") * lax.axis_size("high")
    samples = sample_rows.shape[0]
    scale = 1.0 / math.sqrt(slab * chips * lax.axis_size("core"))
    f32 = jnp.float32
    message = width + 1

    swap = [(0, 1), (1, 0)]
    other = lax.ppermute(panel, "core", swap)
    other_signs = lax.ppermute(signs, "core", swap)

    live, own = pl.pallas_call(
        prepare_kernel,
        in_specs=[SMEM, VMEM, VMEM, VMEM],
        out_shape=(jax.ShapeDtypeStruct((chips, LANES), f32), jax.ShapeDtypeStruct((width, length), f32)),
        compiler_params=PARAMS,
    )(counts, sample_rows.reshape(1, samples), panel, signs.reshape(1, length))

    sent = pl.pallas_call(
        lambda *refs: local_kernel(scale, *refs),
        out_shape=jax.ShapeDtypeStruct((message * chips, LANES), f32),
        scratch_shapes=[pltpu.VMEM((2, width * LOW, LANES), f32)],
        compiler_params=PARAMS,
    )(own, other, other_signs.reshape(1, length), live)

    after, _ = lax.optimization_barrier((counts, other))
    brought, step = paired_counts(after)
    sent, step = lax.optimization_barrier((sent, step))
    got = lax.all_to_all(sent.reshape(message * chips, 1, LANES), CHIP, 0, 0, tiled=True)

    mixed, mask = pl.pallas_call(
        lambda *refs: across_kernel(chips, width, *refs),
        in_specs=[VMEM],
        out_specs=(HBM, HBM),
        out_shape=(pltpu.HBM((chips, width, LANES), f32), pltpu.HBM((chips, LANES), f32)),
        scratch_shapes=[
            pltpu.VMEM((width * chips, LANES), f32),
            pltpu.VMEM((chips, LANES), f32),
            pltpu.SemaphoreType.DMA((width // 8 + 1,)),
        ],
        compiler_params=PARAMS,
    )(got.reshape(message * chips, LANES))

    back = lax.all_to_all(mixed, CHIP, 0, 0, tiled=True)

    steps = 8
    part = pl.pallas_call(
        gram_kernel,
        grid=(steps,),
        in_specs=[
            SMEM,
            pl.BlockSpec((chips // steps, width, LANES), lambda s: (s, 0, 0)),
            pl.BlockSpec((chips // steps, LANES), lambda s: (s, 0)),
        ],
        out_specs=pl.BlockSpec((width + 8, width), lambda s: (0, 0)),
        out_shape=jax.ShapeDtypeStruct((width + 8, width), f32),
        compiler_params=PARAMS,
    )(brought, mixed, mask)
    total = half_sum(part)
    total = total + send(total, lambda w, h, c: (w, h, c ^ 1))
    gram = total[:width] / total[width : width + 1]

    pieces = 4
    out = pl.pallas_call(
        unpack_kernel,
        grid=(pieces,),
        in_specs=[pl.BlockSpec((chips // pieces, width, LANES), lambda s: (s, 0, 0))],
        out_specs=pl.BlockSpec((width, length // pieces), lambda s: (0, s)),
        out_shape=jax.ShapeDtypeStruct((width, length), f32),
        compiler_params=PARAMS,
    )(back)
    return out, gram


def solution(mesh):
    wide, narrow = mesh.devices.shape
    mesh = Mesh(mesh.devices.reshape(wide, narrow // 2, 2), AXES)
    placed = (P(None, AXES), P(AXES), P(AXES), P(AXES))
    return jax.shard_map(
        shards,
        mesh=mesh,
        in_specs=placed,
        out_specs=(P(None, AXES), P()),
        check_vma=False,
    )
```

```python
import math

import jax
import jax.numpy as jnp
from jax import lax
from jax.experimental import pallas as pl
from jax.experimental.pallas import tpu as pltpu
from jax.sharding import Mesh
from jax.sharding import PartitionSpec as P

LOW = 32
HIGH = 128
LANES = 128
FAR = ((8, 6), (4, 5))
CHIP = ("wide", "high")
AXES = ("wide", "high", "core")
SMEM = pl.BlockSpec(memory_space=pltpu.SMEM)
VMEM = pl.BlockSpec(memory_space=pltpu.VMEM)
HBM = pl.BlockSpec(memory_space=pltpu.HBM)
PARAMS = pltpu.CompilerParams(vmem_limit_bytes=32 * 2**20)


def signs_of(i, j, n):
    v = jnp.bitwise_and(i, j)
    shift = 1
    while shift < n.bit_length():
        v = jnp.bitwise_xor(v, jnp.right_shift(v, shift))
        shift *= 2
    return (1 - 2 * jnp.bitwise_and(v, 1)).astype(jnp.float32)


def split(x):
    hi = x.astype(jnp.bfloat16)
    lo = (x - hi.astype(jnp.float32)).astype(jnp.bfloat16)
    return hi, lo


def dot(a, b):
    return jnp.dot(a, b, preferred_element_type=jnp.float32)


def butterfly(vs):
    step = 1
    while step < len(vs):
        out = list(vs)
        for i in range(len(vs)):
            if not i & step:
                out[i] = vs[i] + vs[i | step]
                out[i | step] = vs[i] - vs[i | step]
        vs = out
        step *= 2
    return vs


def prepare_kernel(
    counts_ref, rows_hbm, panel_hbm, signs_hbm, mask_ref, own_ref, rows_ref, panel_ref, signs_ref, sems
):
    width = panel_hbm.shape[0]
    groups = [slice(8 * g, 8 * g + 8) for g in range(width // 8)]
    small = [
        pltpu.make_async_copy(source, target, sems.at[n])
        for n, (source, target) in enumerate(
            ((rows_hbm, rows_ref), (signs_hbm, signs_ref))
        )
    ]
    big = [
        pltpu.make_async_copy(panel_hbm.at[rows, :], panel_ref.at[rows, :], sems.at[2 + g])
        for g, rows in enumerate(groups)
    ]
    for copy in small + big:
        copy.start()
    small[0].wait()
    rows = rows_ref[...]
    samples = rows.shape[1]
    slot = lax.broadcasted_iota(jnp.int32, (1, samples), 1)
    rows = jnp.where(slot < counts_ref[0], rows, -1)
    at = lax.broadcasted_iota(jnp.int32, (HIGH, samples), 0)
    tile = (jnp.right_shift(rows, 7) == at).astype(jnp.float32).astype(jnp.bfloat16)
    inner = (jnp.bitwise_and(rows, HIGH - 1) == at).astype(jnp.float32).astype(jnp.bfloat16)
    mask_ref[...] = lax.dot_general(tile, inner, (((1,), (1,)), ((), ())), preferred_element_type=jnp.float32)
    own_sign = 1 - 2 * lax.axis_index("core")
    small[1].wait()
    sign = (signs_ref[...] * own_sign).astype(jnp.float32)
    for g, rows in enumerate(groups):
        big[g].wait()
        own_ref[rows, :] = panel_ref[rows, :] * sign


def local_kernel(scale, own_ref, other_ref, other_signs_ref, mask_ref, out_ref, x_ref):
    width, length = own_ref.shape
    slab = LOW * HIGH
    i = lax.broadcasted_iota(jnp.int32, (2 * HIGH, HIGH), 0)
    j = lax.broadcasted_iota(jnp.int32, (2 * HIGH, HIGH), 1)
    table = (signs_of(jnp.bitwise_and(i, HIGH - 1), j, HIGH) * scale).astype(jnp.bfloat16)
    per = 8
    for s in range(length // slab):
        for g in range(width // 8):
            vs = []
            for a in range(LOW):
                cols = slice(slab * s + LANES * a, slab * s + LANES * (a + 1))
                rows = slice(8 * g, 8 * g + 8)
                vs.append(own_ref[rows, cols] + other_ref[rows, cols] * other_signs_ref[:, cols].astype(jnp.float32))
            for a, v in enumerate(butterfly(vs)):
                x_ref[s % 2, width * a + 8 * g : width * a + 8 * g + 8, :] = v
        for c in range(LOW // per):
            hi, lo = split(x_ref[s % 2, width * per * c : width * per * (c + 1), :])
            z = dot(jnp.concatenate([hi, lo], axis=1), table)
            for k in range(per):
                t = LOW * s + per * c + k
                row = (width + 1) * t
                out_ref[row : row + width, :] = z[width * k : width * (k + 1), :]
                out_ref[row + width : row + width + 1, :] = mask_ref[t : t + 1, :]


def across_kernel(chips, width, in_ref, out_hbm, mask_hbm, keep_ref, mask_ref, sems):
    i = lax.broadcasted_iota(jnp.int32, (chips, 2 * chips), 0)
    j = lax.broadcasted_iota(jnp.int32, (chips, 2 * chips), 1)
    table = signs_of(i, jnp.where(j < chips, j, j - chips), chips).astype(jnp.bfloat16)
    mask_ref[...] = in_ref[pl.ds(width, chips, stride=width + 1), :]
    copies = [pltpu.make_async_copy(mask_ref, mask_hbm, sems.at[width // 8])]
    copies[0].start()
    tiles = keep_ref.reshape(chips, width, LANES)
    for part in range(width // 8):
        for k in range(8 * part, 8 * part + 8, 2):
            x = jnp.concatenate(
                [in_ref[pl.ds(k + n, chips, stride=width + 1), :] for n in range(2)], axis=1
            )
            y = dot(table, jnp.concatenate(split(x), axis=0))
            for n in range(2):
                keep_ref[pl.ds(k + n, chips, stride=width), :] = y[:, LANES * n : LANES * (n + 1)]
        rows = pl.ds(8 * part, 8)
        copies.append(pltpu.make_async_copy(tiles.at[:, rows, :], out_hbm.at[:, rows, :], sems.at[part]))
        copies[-1].start()
    for copy in copies:
        copy.wait()


def gram_kernel(counts_ref, y_ref, mask_ref, out_ref):
    blocks, width, _ = y_ref.shape

    @pl.when(pl.program_id(0) == 0)
    def _():
        out_ref[:width, :] = jnp.zeros((width, width), jnp.float32)
        out_ref[width:, :] = jnp.full((8, width), counts_ref[0].astype(jnp.float32))

    total = out_ref[:width, :]
    per = 8
    for c in range(0, blocks, per):
        plain = jnp.concatenate([y_ref[d] for d in range(c, c + per)], axis=1)
        masked = jnp.concatenate([y_ref[d] * mask_ref[d : d + 1, :] for d in range(c, c + per)], axis=1)
        a_hi, a_lo = split(masked)
        b_hi, b_lo = split(plain)
        nt = (((1,), (1,)), ((), ()))
        for a, b in ((a_hi, b_hi), (a_hi, b_lo), (a_lo, b_hi)):
            total = total + lax.dot_general(a, b, nt, preferred_element_type=jnp.float32)
    out_ref[:width, :] = total


def unpack_kernel(in_ref, out_ref):
    for t in range(in_ref.shape[0]):
        out_ref[:, LANES * t : LANES * (t + 1)] = in_ref[t]


def send(x, move):
    wide, high, core = (lax.axis_size(axis) for axis in AXES)
    pairs = []
    for w in range(wide):
        for h in range(high):
            for c in range(core):
                to = move(w, h, c)
                if to is not None:
                    pairs.append(((w * high + h) * core + c, (to[0] * high + to[1]) * core + to[2]))
    return lax.ppermute(x, AXES, pairs)


def paired_counts(counts):
    got, side = counts, 0
    for far_w, far_h in FAR:
        got = send(got, lambda w, h, c: (w ^ far_w, h ^ far_h, c) if c else None)
        side ^= far_w
    first = jnp.bitwise_and(lax.axis_index("wide"), side & -side) == 0
    return jnp.where(lax.axis_index("core") == 0, counts, jnp.where(first, counts + got, 0)), got


def half_sum(x):
    x = x + send(x, lambda w, h, c: (w, h, c ^ 1))
    x = x + sum(send(x, lambda w, h, c, n=n: (w, h ^ n, c)) for n in (1, 2, 3))
    x = x + sum(send(x, lambda w, h, c, n=n: (w ^ (n & 1), h ^ (2 * (n & 2)), c)) for n in (1, 2, 3))
    half = lax.axis_size("wide") // 4
    own = jnp.where(lax.axis_index("core") == 0, x, 0.0)
    for step in range(half):
        own = own + send(
            x,
            lambda w, h, c, step=step: (w ^ (2 * (step + half * c)), h, c) if step + c else None,
        )
    return own


def shards(panel, signs, sample_rows, counts):
    width, length = panel.shape
    slab = LOW * HIGH
    chips = lax.axis_size("wide") * lax.axis_size("high")
    samples = sample_rows.shape[0]
    scale = 1.0 / math.sqrt(slab * chips * lax.axis_size("core"))
    f32 = jnp.float32
    message = width + 1

    swap = [(0, 1), (1, 0)]
    other = lax.ppermute(panel, "core", swap)
    other_signs = lax.ppermute(signs, "core", swap)

    inputs = (sample_rows.reshape(1, samples), panel, signs.reshape(1, length))
    live, own = pl.pallas_call(
        prepare_kernel,
        in_specs=[SMEM] + [HBM] * 3,
        out_specs=(VMEM, VMEM),
        out_shape=(jax.ShapeDtypeStruct((chips, LANES), f32), jax.ShapeDtypeStruct((width, length), f32)),
        scratch_shapes=[
            pltpu.VMEM((1, samples), jnp.int32),
            pltpu.VMEM((width, length), f32),
            pltpu.VMEM((1, length), jnp.int32),
            pltpu.SemaphoreType.DMA((width // 8 + 2,)),
        ],
        compiler_params=PARAMS,
    )(counts, *(pltpu.with_memory_space_constraint(x, pltpu.HBM) for x in inputs))

    after, own = lax.optimization_barrier((counts, own))
    brought, step = paired_counts(after)

    sent = pl.pallas_call(
        lambda *refs: local_kernel(scale, *refs),
        out_shape=jax.ShapeDtypeStruct((message * chips, LANES), f32),
        scratch_shapes=[pltpu.VMEM((2, width * LOW, LANES), f32)],
        compiler_params=PARAMS,
    )(own, other, other_signs.reshape(1, length), live)

    sent, step = lax.optimization_barrier((sent, step))
    got = lax.all_to_all(sent.reshape(message * chips, 1, LANES), CHIP, 0, 0, tiled=True)

    mixed, mask = pl.pallas_call(
        lambda *refs: across_kernel(chips, width, *refs),
        in_specs=[VMEM],
        out_specs=(HBM, HBM),
        out_shape=(pltpu.HBM((chips, width, LANES), f32), pltpu.HBM((chips, LANES), f32)),
        scratch_shapes=[
            pltpu.VMEM((width * chips, LANES), f32),
            pltpu.VMEM((chips, LANES), f32),
            pltpu.SemaphoreType.DMA((width // 8 + 1,)),
        ],
        compiler_params=PARAMS,
    )(got.reshape(message * chips, LANES))

    back = lax.all_to_all(mixed, CHIP, 0, 0, tiled=True)

    steps = 8
    part = pl.pallas_call(
        gram_kernel,
        grid=(steps,),
        in_specs=[
            SMEM,
            pl.BlockSpec((chips // steps, width, LANES), lambda s: (s, 0, 0)),
            pl.BlockSpec((chips // steps, LANES), lambda s: (s, 0)),
        ],
        out_specs=pl.BlockSpec((width + 8, width), lambda s: (0, 0)),
        out_shape=jax.ShapeDtypeStruct((width + 8, width), f32),
        compiler_params=PARAMS,
    )(brought, mixed, mask)
    total = half_sum(part)
    total = total + send(total, lambda w, h, c: (w, h, c ^ 1))
    gram = total[:width] / total[width : width + 1]

    pieces = 4
    out = pl.pallas_call(
        unpack_kernel,
        grid=(pieces,),
        in_specs=[pl.BlockSpec((chips // pieces, width, LANES), lambda s: (s, 0, 0))],
        out_specs=pl.BlockSpec((width, length // pieces), lambda s: (0, s)),
        out_shape=jax.ShapeDtypeStruct((width, length), f32),
        compiler_params=PARAMS,
    )(back)
    return out, gram


def solution(mesh):
    wide, narrow = mesh.devices.shape
    mesh = Mesh(mesh.devices.reshape(wide, narrow // 2, 2), AXES)
    placed = (P(None, AXES), P(AXES), P(AXES), P(AXES))
    return jax.shard_map(
        shards,
        mesh=mesh,
        in_specs=placed,
        out_specs=(P(None, AXES), P()),
        check_vma=False,
    )
```

```python
import math

import jax
import jax.numpy as jnp
from jax import lax
from jax.experimental import pallas as pl
from jax.experimental.pallas import tpu as pltpu
from jax.sharding import Mesh
from jax.sharding import PartitionSpec as P

LOW = 32
HIGH = 128
LANES = 128
FAR = ((8, 6), (4, 6))
CHIP = ("wide", "high")
AXES = ("wide", "high", "core")
SMEM = pl.BlockSpec(memory_space=pltpu.SMEM)
VMEM = pl.BlockSpec(memory_space=pltpu.VMEM)
HBM = pl.BlockSpec(memory_space=pltpu.HBM)
PARAMS = pltpu.CompilerParams(vmem_limit_bytes=32 * 2**20)


def signs_of(i, j, n):
    v = jnp.bitwise_and(i, j)
    shift = 1
    while shift < n.bit_length():
        v = jnp.bitwise_xor(v, jnp.right_shift(v, shift))
        shift *= 2
    return (1 - 2 * jnp.bitwise_and(v, 1)).astype(jnp.float32)


def split(x):
    hi = x.astype(jnp.bfloat16)
    lo = (x - hi.astype(jnp.float32)).astype(jnp.bfloat16)
    return hi, lo


def dot(a, b):
    return jnp.dot(a, b, preferred_element_type=jnp.float32)


def butterfly(vs):
    step = 1
    while step < len(vs):
        out = list(vs)
        for i in range(len(vs)):
            if not i & step:
                out[i] = vs[i] + vs[i | step]
                out[i | step] = vs[i] - vs[i | step]
        vs = out
        step *= 2
    return vs


def prepare_kernel(
    counts_ref, rows_hbm, panel_hbm, signs_hbm, mask_ref, own_ref, rows_ref, panel_ref, signs_ref, sems
):
    width = panel_hbm.shape[0]
    groups = [slice(8 * g, 8 * g + 8) for g in range(width // 8)]
    small = [
        pltpu.make_async_copy(source, target, sems.at[n])
        for n, (source, target) in enumerate(
            ((rows_hbm, rows_ref), (signs_hbm, signs_ref))
        )
    ]
    big = [
        pltpu.make_async_copy(panel_hbm.at[rows, :], panel_ref.at[rows, :], sems.at[2 + g])
        for g, rows in enumerate(groups)
    ]
    for copy in small + big:
        copy.start()
    small[0].wait()
    rows = rows_ref[...]
    samples = rows.shape[1]
    slot = lax.broadcasted_iota(jnp.int32, (1, samples), 1)
    rows = jnp.where(slot < counts_ref[0], rows, -1)
    at = lax.broadcasted_iota(jnp.int32, (HIGH, samples), 0)
    tile = (jnp.right_shift(rows, 7) == at).astype(jnp.float32).astype(jnp.bfloat16)
    inner = (jnp.bitwise_and(rows, HIGH - 1) == at).astype(jnp.float32).astype(jnp.bfloat16)
    mask_ref[...] = lax.dot_general(tile, inner, (((1,), (1,)), ((), ())), preferred_element_type=jnp.float32)
    own_sign = 1 - 2 * lax.axis_index("core")
    small[1].wait()
    sign = (signs_ref[...] * own_sign).astype(jnp.float32)
    for g, rows in enumerate(groups):
        big[g].wait()
        own_ref[rows, :] = panel_ref[rows, :] * sign


def local_kernel(scale, own_ref, other_ref, other_signs_ref, mask_ref, out_ref, x_ref):
    width, length = own_ref.shape
    slab = LOW * HIGH
    i = lax.broadcasted_iota(jnp.int32, (2 * HIGH, HIGH), 0)
    j = lax.broadcasted_iota(jnp.int32, (2 * HIGH, HIGH), 1)
    table = (signs_of(jnp.bitwise_and(i, HIGH - 1), j, HIGH) * scale).astype(jnp.bfloat16)
    per = 8
    for s in range(length // slab):
        for g in range(width // 8):
            vs = []
            for a in range(LOW):
                cols = slice(slab * s + LANES * a, slab * s + LANES * (a + 1))
                rows = slice(8 * g, 8 * g + 8)
                vs.append(own_ref[rows, cols] + other_ref[rows, cols] * other_signs_ref[:, cols].astype(jnp.float32))
            for a, v in enumerate(butterfly(vs)):
                x_ref[s % 2, width * a + 8 * g : width * a + 8 * g + 8, :] = v
        for c in range(LOW // per):
            hi, lo = split(x_ref[s % 2, width * per * c : width * per * (c + 1), :])
            z = dot(jnp.concatenate([hi, lo], axis=1), table)
            for k in range(per):
                t = LOW * s + per * c + k
                row = (width + 1) * t
                out_ref[row : row + width, :] = z[width * k : width * (k + 1), :]
                out_ref[row + width : row + width + 1, :] = mask_ref[t : t + 1, :]


def across_kernel(chips, width, in_ref, out_hbm, mask_hbm, keep_ref, mask_ref, sems):
    i = lax.broadcasted_iota(jnp.int32, (chips, 2 * chips), 0)
    j = lax.broadcasted_iota(jnp.int32, (chips, 2 * chips), 1)
    table = signs_of(i, jnp.where(j < chips, j, j - chips), chips).astype(jnp.bfloat16)
    mask_ref[...] = in_ref[pl.ds(width, chips, stride=width + 1), :]
    copies = [pltpu.make_async_copy(mask_ref, mask_hbm, sems.at[width // 8])]
    copies[0].start()
    tiles = keep_ref.reshape(chips, width, LANES)
    for part in range(width // 8):
        for k in range(8 * part, 8 * part + 8, 2):
            x = jnp.concatenate(
                [in_ref[pl.ds(k + n, chips, stride=width + 1), :] for n in range(2)], axis=1
            )
            y = dot(table, jnp.concatenate(split(x), axis=0))
            for n in range(2):
                keep_ref[pl.ds(k + n, chips, stride=width), :] = y[:, LANES * n : LANES * (n + 1)]
        rows = pl.ds(8 * part, 8)
        copies.append(pltpu.make_async_copy(tiles.at[:, rows, :], out_hbm.at[:, rows, :], sems.at[part]))
        copies[-1].start()
    for copy in copies:
        copy.wait()


def gram_kernel(counts_ref, y_hbm, mask_hbm, out_ref, y_ref, mask_ref, sems):
    blocks, width, _ = y_hbm.shape
    parts = sems.shape[0] - 1
    step = blocks // parts
    copies = [pltpu.make_async_copy(mask_hbm, mask_ref, sems.at[parts])]
    for n in range(parts):
        rows = pl.ds(step * n, step)
        copies.append(pltpu.make_async_copy(y_hbm.at[rows], y_ref.at[rows], sems.at[n]))
    for copy in copies:
        copy.start()
    copies[0].wait()
    total = jnp.zeros((width, width), jnp.float32)
    per = 8
    nt = (((1,), (1,)), ((), ()))
    for c in range(0, blocks, per):
        if c % step == 0:
            copies[1 + c // step].wait()
        plain = jnp.concatenate([y_ref[d] for d in range(c, c + per)], axis=1)
        masked = jnp.concatenate([y_ref[d] * mask_ref[d : d + 1, :] for d in range(c, c + per)], axis=1)
        a_hi, a_lo = split(masked)
        b_hi, b_lo = split(plain)
        for a, b in ((a_hi, b_hi), (a_hi, b_lo), (a_lo, b_hi)):
            total = total + lax.dot_general(a, b, nt, preferred_element_type=jnp.float32)
    out_ref[:width, :] = total
    out_ref[width:, :] = jnp.full((8, width), counts_ref[0].astype(jnp.float32))


def unpack_kernel(in_ref, out_ref):
    for t in range(in_ref.shape[0]):
        out_ref[:, LANES * t : LANES * (t + 1)] = in_ref[t]


def send(x, move):
    wide, high, core = (lax.axis_size(axis) for axis in AXES)
    pairs = []
    for w in range(wide):
        for h in range(high):
            for c in range(core):
                to = move(w, h, c)
                if to is not None:
                    pairs.append(((w * high + h) * core + c, (to[0] * high + to[1]) * core + to[2]))
    return lax.ppermute(x, AXES, pairs)


def paired_counts(counts):
    got, side = counts, 0
    for far_w, far_h in FAR:
        got = send(got, lambda w, h, c: (w ^ far_w, h ^ far_h, c) if c else None)
        side ^= far_w
    first = jnp.bitwise_and(lax.axis_index("wide"), side & -side) == 0
    return jnp.where(lax.axis_index("core") == 0, counts, jnp.where(first, counts + got, 0)), got


def half_sum(x):
    x = x + send(x, lambda w, h, c: (w, h, c ^ 1))
    x = x + sum(send(x, lambda w, h, c, n=n: (w, h ^ n, c)) for n in (1, 2, 3))
    x = x + sum(send(x, lambda w, h, c, n=n: (w ^ (n & 1), h ^ (2 * (n & 2)), c)) for n in (1, 2, 3))
    half = lax.axis_size("wide") // 4
    own = jnp.where(lax.axis_index("core") == 0, x, 0.0)
    for step in range(half):
        own = own + send(
            x,
            lambda w, h, c, step=step: (w ^ (2 * (step + half * c)), h, c) if step + c else None,
        )
    return own


def shards(panel, signs, sample_rows, counts):
    width, length = panel.shape
    slab = LOW * HIGH
    chips = lax.axis_size("wide") * lax.axis_size("high")
    samples = sample_rows.shape[0]
    scale = 1.0 / math.sqrt(slab * chips * lax.axis_size("core"))
    f32 = jnp.float32
    message = width + 1

    swap = [(0, 1), (1, 0)]
    other = lax.ppermute(panel, "core", swap)
    other_signs = lax.ppermute(signs, "core", swap)

    inputs = (sample_rows.reshape(1, samples), panel, signs.reshape(1, length))
    live, own = pl.pallas_call(
        prepare_kernel,
        in_specs=[SMEM] + [HBM] * 3,
        out_specs=(VMEM, VMEM),
        out_shape=(jax.ShapeDtypeStruct((chips, LANES), f32), jax.ShapeDtypeStruct((width, length), f32)),
        scratch_shapes=[
            pltpu.VMEM((1, samples), jnp.int32),
            pltpu.VMEM((width, length), f32),
            pltpu.VMEM((1, length), jnp.int32),
            pltpu.SemaphoreType.DMA((width // 8 + 2,)),
        ],
        compiler_params=PARAMS,
    )(counts, *(pltpu.with_memory_space_constraint(x, pltpu.HBM) for x in inputs))

    after, own = lax.optimization_barrier((counts, own))
    brought, step = paired_counts(after)

    sent = pl.pallas_call(
        lambda *refs: local_kernel(scale, *refs),
        out_shape=jax.ShapeDtypeStruct((message * chips, LANES), f32),
        scratch_shapes=[pltpu.VMEM((2, width * LOW, LANES), f32)],
        compiler_params=PARAMS,
    )(own, other, other_signs.reshape(1, length), live)

    sent, step = lax.optimization_barrier((sent, step))
    got = lax.all_to_all(sent.reshape(message * chips, 1, LANES), CHIP, 0, 0, tiled=True)

    mixed, mask = pl.pallas_call(
        lambda *refs: across_kernel(chips, width, *refs),
        in_specs=[VMEM],
        out_specs=(HBM, HBM),
        out_shape=(pltpu.HBM((chips, width, LANES), f32), pltpu.HBM((chips, LANES), f32)),
        scratch_shapes=[
            pltpu.VMEM((width * chips, LANES), f32),
            pltpu.VMEM((chips, LANES), f32),
            pltpu.SemaphoreType.DMA((width // 8 + 1,)),
        ],
        compiler_params=PARAMS,
    )(got.reshape(message * chips, LANES))

    back = lax.all_to_all(mixed, CHIP, 0, 0, tiled=True)

    part = pl.pallas_call(
        gram_kernel,
        in_specs=[SMEM, HBM, HBM],
        out_specs=VMEM,
        out_shape=jax.ShapeDtypeStruct((width + 8, width), f32),
        scratch_shapes=[
            pltpu.VMEM((chips, width, LANES), f32),
            pltpu.VMEM((chips, LANES), f32),
            pltpu.SemaphoreType.DMA((9,)),
        ],
        compiler_params=PARAMS,
    )(brought, *(pltpu.with_memory_space_constraint(x, pltpu.HBM) for x in (mixed, mask)))
    total = half_sum(part)
    total = total + send(total, lambda w, h, c: (w, h, c ^ 1))
    gram = total[:width] / total[width : width + 1]

    pieces = 4
    out = pl.pallas_call(
        unpack_kernel,
        grid=(pieces,),
        in_specs=[pl.BlockSpec((chips // pieces, width, LANES), lambda s: (s, 0, 0))],
        out_specs=pl.BlockSpec((width, length // pieces), lambda s: (0, s)),
        out_shape=jax.ShapeDtypeStruct((width, length), f32),
        compiler_params=PARAMS,
    )(back)
    return out, gram


def solution(mesh):
    wide, narrow = mesh.devices.shape
    mesh = Mesh(mesh.devices.reshape(wide, narrow // 2, 2), AXES)
    placed = (P(None, AXES), P(AXES), P(AXES), P(AXES))
    return jax.shard_map(
        shards,
        mesh=mesh,
        in_specs=placed,
        out_specs=(P(None, AXES), P()),
        check_vma=False,
    )
```

```python
import math

import jax
import jax.numpy as jnp
from jax import lax
from jax.experimental import pallas as pl
from jax.experimental.pallas import tpu as pltpu
from jax.sharding import Mesh
from jax.sharding import PartitionSpec as P

LOW = 32
HIGH = 128
LANES = 128
FAR = ((8, 6), (4, 6))
CHIP = ("wide", "high")
AXES = ("wide", "high", "core")
SMEM = pl.BlockSpec(memory_space=pltpu.SMEM)
VMEM = pl.BlockSpec(memory_space=pltpu.VMEM)
HBM = pl.BlockSpec(memory_space=pltpu.HBM)
PARAMS = pltpu.CompilerParams(vmem_limit_bytes=32 * 2**20)


def signs_of(i, j, n):
    v = jnp.bitwise_and(i, j)
    shift = 1
    while shift < n.bit_length():
        v = jnp.bitwise_xor(v, jnp.right_shift(v, shift))
        shift *= 2
    return (1 - 2 * jnp.bitwise_and(v, 1)).astype(jnp.float32)


def split(x):
    hi = x.astype(jnp.bfloat16)
    lo = (x - hi.astype(jnp.float32)).astype(jnp.bfloat16)
    return hi, lo


def dot(a, b):
    return jnp.dot(a, b, preferred_element_type=jnp.float32)


def butterfly(vs):
    step = 1
    while step < len(vs):
        out = list(vs)
        for i in range(len(vs)):
            if not i & step:
                out[i] = vs[i] + vs[i | step]
                out[i | step] = vs[i] - vs[i | step]
        vs = out
        step *= 2
    return vs


def prepare_kernel(
    counts_ref, rows_hbm, panel_hbm, signs_hbm, mask_ref, own_ref, rows_ref, panel_ref, signs_ref, sems
):
    width = panel_hbm.shape[0]
    groups = [slice(8 * g, 8 * g + 8) for g in range(width // 8)]
    small = [
        pltpu.make_async_copy(source, target, sems.at[n])
        for n, (source, target) in enumerate(
            ((rows_hbm, rows_ref), (signs_hbm, signs_ref))
        )
    ]
    big = [
        pltpu.make_async_copy(panel_hbm.at[rows, :], panel_ref.at[rows, :], sems.at[2 + g])
        for g, rows in enumerate(groups)
    ]
    for copy in small + big:
        copy.start()
    small[0].wait()
    rows = rows_ref[...]
    samples = rows.shape[1]
    slot = lax.broadcasted_iota(jnp.int32, (1, samples), 1)
    rows = jnp.where(slot < counts_ref[0], rows, -1)
    at = lax.broadcasted_iota(jnp.int32, (HIGH, samples), 0)
    tile = (jnp.right_shift(rows, 7) == at).astype(jnp.float32).astype(jnp.bfloat16)
    inner = (jnp.bitwise_and(rows, HIGH - 1) == at).astype(jnp.float32).astype(jnp.bfloat16)
    mask_ref[...] = lax.dot_general(tile, inner, (((1,), (1,)), ((), ())), preferred_element_type=jnp.float32)
    own_sign = 1 - 2 * lax.axis_index("core")
    small[1].wait()
    sign = (signs_ref[...] * own_sign).astype(jnp.float32)
    for g, rows in enumerate(groups):
        big[g].wait()
        own_ref[rows, :] = panel_ref[rows, :] * sign


def local_kernel(scale, own_ref, other_ref, other_signs_ref, mask_ref, out_ref, x_ref):
    width, length = own_ref.shape
    slab = LOW * HIGH
    i = lax.broadcasted_iota(jnp.int32, (2 * HIGH, HIGH), 0)
    j = lax.broadcasted_iota(jnp.int32, (2 * HIGH, HIGH), 1)
    table = (signs_of(jnp.bitwise_and(i, HIGH - 1), j, HIGH) * scale).astype(jnp.bfloat16)
    per = 8
    for s in range(length // slab):
        for g in range(width // 8):
            vs = []
            for a in range(LOW):
                cols = slice(slab * s + LANES * a, slab * s + LANES * (a + 1))
                rows = slice(8 * g, 8 * g + 8)
                vs.append(own_ref[rows, cols] + other_ref[rows, cols] * other_signs_ref[:, cols].astype(jnp.float32))
            for a, v in enumerate(butterfly(vs)):
                x_ref[s % 2, width * a + 8 * g : width * a + 8 * g + 8, :] = v
        for c in range(LOW // per):
            hi, lo = split(x_ref[s % 2, width * per * c : width * per * (c + 1), :])
            z = dot(jnp.concatenate([hi, lo], axis=1), table)
            for k in range(per):
                t = LOW * s + per * c + k
                row = (width + 1) * t
                out_ref[row : row + width, :] = z[width * k : width * (k + 1), :]
                out_ref[row + width : row + width + 1, :] = mask_ref[t : t + 1, :]


def across_kernel(chips, width, in_ref, out_hbm, mask_hbm, keep_ref, mask_ref, sems):
    i = lax.broadcasted_iota(jnp.int32, (chips, 2 * chips), 0)
    j = lax.broadcasted_iota(jnp.int32, (chips, 2 * chips), 1)
    table = signs_of(i, jnp.where(j < chips, j, j - chips), chips).astype(jnp.bfloat16)
    mask_ref[...] = in_ref[pl.ds(width, chips, stride=width + 1), :]
    copies = [pltpu.make_async_copy(mask_ref, mask_hbm, sems.at[width // 8])]
    copies[0].start()
    tiles = keep_ref.reshape(chips, width, LANES)
    for part in range(width // 8):
        for k in range(8 * part, 8 * part + 8, 2):
            x = jnp.concatenate(
                [in_ref[pl.ds(k + n, chips, stride=width + 1), :] for n in range(2)], axis=1
            )
            y = dot(table, jnp.concatenate(split(x), axis=0))
            for n in range(2):
                keep_ref[pl.ds(k + n, chips, stride=width), :] = y[:, LANES * n : LANES * (n + 1)]
        rows = pl.ds(8 * part, 8)
        copies.append(pltpu.make_async_copy(tiles.at[:, rows, :], out_hbm.at[:, rows, :], sems.at[part]))
        copies[-1].start()
    for copy in copies:
        copy.wait()


def gram_kernel(counts_ref, y_hbm, mask_hbm, out_ref, y_ref, mask_ref, sems):
    blocks, width, _ = y_hbm.shape
    parts = sems.shape[0] - 1
    step = blocks // parts
    copies = [pltpu.make_async_copy(mask_hbm, mask_ref, sems.at[parts])]
    for n in range(parts):
        rows = pl.ds(step * n, step)
        copies.append(pltpu.make_async_copy(y_hbm.at[rows], y_ref.at[rows], sems.at[n]))
    for copy in copies:
        copy.start()
    copies[0].wait()
    total = jnp.zeros((width, width), jnp.float32)
    per = 8
    nt = (((1,), (1,)), ((), ()))
    for c in range(0, blocks, per):
        if c % step == 0:
            copies[1 + c // step].wait()
        plain = jnp.concatenate([y_ref[d] for d in range(c, c + per)], axis=1)
        masked = jnp.concatenate([y_ref[d] * mask_ref[d : d + 1, :] for d in range(c, c + per)], axis=1)
        a_hi, a_lo = split(masked)
        b_hi, b_lo = split(plain)
        for a, b in ((a_hi, b_hi), (a_hi, b_lo), (a_lo, b_hi)):
            total = total + lax.dot_general(a, b, nt, preferred_element_type=jnp.float32)
    out_ref[:width, :] = total
    out_ref[width:, :] = jnp.full((8, width), counts_ref[0].astype(jnp.float32))


def unpack_kernel(in_ref, out_hbm, keep_ref, sems):
    chips = in_ref.shape[0]
    pieces = sems.shape[0]
    copies = []
    for n in range(pieces):
        for t in range(chips // pieces * n, chips // pieces * (n + 1)):
            keep_ref[:, LANES * t : LANES * (t + 1)] = in_ref[t]
        cols = pl.ds(LANES * (chips // pieces) * n, LANES * (chips // pieces))
        copies.append(pltpu.make_async_copy(keep_ref.at[:, cols], out_hbm.at[:, cols], sems.at[n]))
        copies[-1].start()
    for copy in copies:
        copy.wait()


def send(x, move):
    wide, high, core = (lax.axis_size(axis) for axis in AXES)
    pairs = []
    for w in range(wide):
        for h in range(high):
            for c in range(core):
                to = move(w, h, c)
                if to is not None:
                    pairs.append(((w * high + h) * core + c, (to[0] * high + to[1]) * core + to[2]))
    return lax.ppermute(x, AXES, pairs)


def paired_counts(counts):
    got, side = counts, 0
    for far_w, far_h in FAR:
        got = send(got, lambda w, h, c: (w ^ far_w, h ^ far_h, c) if c else None)
        side ^= far_w
    first = jnp.bitwise_and(lax.axis_index("wide"), side & -side) == 0
    return jnp.where(lax.axis_index("core") == 0, counts, jnp.where(first, counts + got, 0)), got


def half_sum(x):
    x = x + send(x, lambda w, h, c: (w, h, c ^ 1))
    x = x + sum(send(x, lambda w, h, c, n=n: (w, h ^ n, c)) for n in (1, 2, 3))
    x = x + sum(send(x, lambda w, h, c, n=n: (w ^ (n & 1), h ^ (2 * (n & 2)), c)) for n in (1, 2, 3))
    half = lax.axis_size("wide") // 4
    own = jnp.where(lax.axis_index("core") == 0, x, 0.0)
    for step in range(half):
        own = own + send(
            x,
            lambda w, h, c, step=step: (w ^ (2 * (step + half * c)), h, c) if step + c else None,
        )
    return own


def shards(panel, signs, sample_rows, counts):
    width, length = panel.shape
    slab = LOW * HIGH
    chips = lax.axis_size("wide") * lax.axis_size("high")
    samples = sample_rows.shape[0]
    scale = 1.0 / math.sqrt(slab * chips * lax.axis_size("core"))
    f32 = jnp.float32
    message = width + 1

    swap = [(0, 1), (1, 0)]
    other = lax.ppermute(panel, "core", swap)
    other_signs = lax.ppermute(signs, "core", swap)

    inputs = (sample_rows.reshape(1, samples), panel, signs.reshape(1, length))
    live, own = pl.pallas_call(
        prepare_kernel,
        in_specs=[SMEM] + [HBM] * 3,
        out_specs=(VMEM, VMEM),
        out_shape=(jax.ShapeDtypeStruct((chips, LANES), f32), jax.ShapeDtypeStruct((width, length), f32)),
        scratch_shapes=[
            pltpu.VMEM((1, samples), jnp.int32),
            pltpu.VMEM((width, length), f32),
            pltpu.VMEM((1, length), jnp.int32),
            pltpu.SemaphoreType.DMA((width // 8 + 2,)),
        ],
        compiler_params=PARAMS,
    )(counts, *(pltpu.with_memory_space_constraint(x, pltpu.HBM) for x in inputs))

    after, own = lax.optimization_barrier((counts, own))
    brought, step = paired_counts(after)

    sent = pl.pallas_call(
        lambda *refs: local_kernel(scale, *refs),
        out_shape=jax.ShapeDtypeStruct((message * chips, LANES), f32),
        scratch_shapes=[pltpu.VMEM((2, width * LOW, LANES), f32)],
        compiler_params=PARAMS,
    )(own, other, other_signs.reshape(1, length), live)

    sent, step = lax.optimization_barrier((sent, step))
    got = lax.all_to_all(sent.reshape(message * chips, 1, LANES), CHIP, 0, 0, tiled=True)

    mixed, mask = pl.pallas_call(
        lambda *refs: across_kernel(chips, width, *refs),
        in_specs=[VMEM],
        out_specs=(HBM, HBM),
        out_shape=(pltpu.HBM((chips, width, LANES), f32), pltpu.HBM((chips, LANES), f32)),
        scratch_shapes=[
            pltpu.VMEM((width * chips, LANES), f32),
            pltpu.VMEM((chips, LANES), f32),
            pltpu.SemaphoreType.DMA((width // 8 + 1,)),
        ],
        compiler_params=PARAMS,
    )(got.reshape(message * chips, LANES))

    back = lax.all_to_all(mixed, CHIP, 0, 0, tiled=True)

    part = pl.pallas_call(
        gram_kernel,
        in_specs=[SMEM, HBM, HBM],
        out_specs=VMEM,
        out_shape=jax.ShapeDtypeStruct((width + 8, width), f32),
        scratch_shapes=[
            pltpu.VMEM((chips, width, LANES), f32),
            pltpu.VMEM((chips, LANES), f32),
            pltpu.SemaphoreType.DMA((9,)),
        ],
        compiler_params=PARAMS,
    )(brought, *(pltpu.with_memory_space_constraint(x, pltpu.HBM) for x in (mixed, mask)))
    total = half_sum(part)
    total = total + send(total, lambda w, h, c: (w, h, c ^ 1))
    gram = total[:width] / total[width : width + 1]

    out = pl.pallas_call(
        unpack_kernel,
        in_specs=[VMEM],
        out_specs=HBM,
        out_shape=pltpu.HBM((width, length), f32),
        scratch_shapes=[pltpu.VMEM((width, length), f32), pltpu.SemaphoreType.DMA((8,))],
        compiler_params=PARAMS,
    )(back)
    return out, gram


def solution(mesh):
    wide, narrow = mesh.devices.shape
    mesh = Mesh(mesh.devices.reshape(wide, narrow // 2, 2), AXES)
    placed = (P(None, AXES), P(AXES), P(AXES), P(AXES))
    return jax.shard_map(
        shards,
        mesh=mesh,
        in_specs=placed,
        out_specs=(P(None, AXES), P()),
        check_vma=False,
    )
```

```python
import math

import jax
import jax.numpy as jnp
from jax import lax
from jax.experimental import pallas as pl
from jax.experimental.pallas import tpu as pltpu
from jax.sharding import Mesh
from jax.sharding import PartitionSpec as P

LOW = 32
HIGH = 128
LANES = 128
FAR = ((8, 6), (4, 6))
CHIP = ("wide", "high")
AXES = ("wide", "high", "core")
SMEM = pl.BlockSpec(memory_space=pltpu.SMEM)
VMEM = pl.BlockSpec(memory_space=pltpu.VMEM)
HBM = pl.BlockSpec(memory_space=pltpu.HBM)
PARAMS = pltpu.CompilerParams(vmem_limit_bytes=32 * 2**20)


def signs_of(i, j, n):
    v = jnp.bitwise_and(i, j)
    shift = 1
    while shift < n.bit_length():
        v = jnp.bitwise_xor(v, jnp.right_shift(v, shift))
        shift *= 2
    return (1 - 2 * jnp.bitwise_and(v, 1)).astype(jnp.float32)


def split(x):
    hi = x.astype(jnp.bfloat16)
    lo = (x - hi.astype(jnp.float32)).astype(jnp.bfloat16)
    return hi, lo


def dot(a, b):
    return jnp.dot(a, b, preferred_element_type=jnp.float32)


def butterfly(vs):
    step = 1
    while step < len(vs):
        out = list(vs)
        for i in range(len(vs)):
            if not i & step:
                out[i] = vs[i] + vs[i | step]
                out[i | step] = vs[i] - vs[i | step]
        vs = out
        step *= 2
    return vs


def prepare_kernel(
    counts_ref, rows_hbm, panel_hbm, signs_hbm, mask_ref, own_ref, rows_ref, panel_ref, signs_ref, sems
):
    width = panel_hbm.shape[0]
    groups = [slice(8 * g, 8 * g + 8) for g in range(width // 8)]
    small = [
        pltpu.make_async_copy(source, target, sems.at[n])
        for n, (source, target) in enumerate(
            ((rows_hbm, rows_ref), (signs_hbm, signs_ref))
        )
    ]
    big = [
        pltpu.make_async_copy(panel_hbm.at[rows, :], panel_ref.at[rows, :], sems.at[2 + g])
        for g, rows in enumerate(groups)
    ]
    for copy in small + big:
        copy.start()
    small[0].wait()
    rows = rows_ref[...]
    samples = rows.shape[1]
    slot = lax.broadcasted_iota(jnp.int32, (1, samples), 1)
    rows = jnp.where(slot < counts_ref[0], rows, -1)
    at = lax.broadcasted_iota(jnp.int32, (HIGH, samples), 0)
    tile = (jnp.right_shift(rows, 7) == at).astype(jnp.float32).astype(jnp.bfloat16)
    inner = (jnp.bitwise_and(rows, HIGH - 1) == at).astype(jnp.float32).astype(jnp.bfloat16)
    mask_ref[...] = lax.dot_general(tile, inner, (((1,), (1,)), ((), ())), preferred_element_type=jnp.float32)
    own_sign = 1 - 2 * lax.axis_index("core")
    small[1].wait()
    sign = (signs_ref[...] * own_sign).astype(jnp.float32)
    for g, rows in enumerate(groups):
        big[g].wait()
        own_ref[rows, :] = panel_ref[rows, :] * sign


def local_kernel(scale, own_ref, other_ref, other_signs_ref, mask_ref, out_ref, x_ref):
    width, length = own_ref.shape
    slab = LOW * HIGH
    i = lax.broadcasted_iota(jnp.int32, (2 * HIGH, HIGH), 0)
    j = lax.broadcasted_iota(jnp.int32, (2 * HIGH, HIGH), 1)
    table = (signs_of(jnp.bitwise_and(i, HIGH - 1), j, HIGH) * scale).astype(jnp.bfloat16)
    per = 8
    for s in range(length // slab):
        for g in range(width // 8):
            vs = []
            for a in range(LOW):
                cols = slice(slab * s + LANES * a, slab * s + LANES * (a + 1))
                rows = slice(8 * g, 8 * g + 8)
                vs.append(own_ref[rows, cols] + other_ref[rows, cols] * other_signs_ref[:, cols].astype(jnp.float32))
            for a, v in enumerate(butterfly(vs)):
                x_ref[s % 2, width * a + 8 * g : width * a + 8 * g + 8, :] = v
        for c in range(LOW // per):
            hi, lo = split(x_ref[s % 2, width * per * c : width * per * (c + 1), :])
            z = dot(jnp.concatenate([hi, lo], axis=1), table)
            for k in range(per):
                t = LOW * s + per * c + k
                row = (width + 1) * t
                out_ref[row : row + width, :] = z[width * k : width * (k + 1), :]
                out_ref[row + width : row + width + 1, :] = mask_ref[t : t + 1, :]


def across_kernel(chips, width, in_ref, out_hbm, mask_hbm, keep_ref, mask_ref, sems):
    i = lax.broadcasted_iota(jnp.int32, (chips, 2 * chips), 0)
    j = lax.broadcasted_iota(jnp.int32, (chips, 2 * chips), 1)
    table = signs_of(i, jnp.where(j < chips, j, j - chips), chips).astype(jnp.bfloat16)
    copies = []
    tiles = keep_ref.reshape(chips, width, LANES)
    for part in range(width // 8):
        for k in range(8 * part, 8 * part + 8, 2):
            x = jnp.concatenate(
                [in_ref[pl.ds(k + n, chips, stride=width + 1), :] for n in range(2)], axis=1
            )
            y = dot(table, jnp.concatenate(split(x), axis=0))
            for n in range(2):
                keep_ref[pl.ds(k + n, chips, stride=width), :] = y[:, LANES * n : LANES * (n + 1)]
        rows = pl.ds(8 * part, 8)
        copies.append(pltpu.make_async_copy(tiles.at[:, rows, :], out_hbm.at[:, rows, :], sems.at[part]))
        copies[-1].start()
    mask_ref[...] = in_ref[pl.ds(width, chips, stride=width + 1), :]
    copies.append(pltpu.make_async_copy(mask_ref, mask_hbm, sems.at[width // 8]))
    copies[-1].start()
    for copy in copies:
        copy.wait()


def gram_kernel(counts_ref, y_hbm, mask_hbm, out_ref, y_ref, mask_ref, sems):
    blocks, width, _ = y_hbm.shape
    parts = sems.shape[0] - 1
    step = blocks // parts
    copies = [pltpu.make_async_copy(mask_hbm, mask_ref, sems.at[parts])]
    for n in range(parts):
        rows = pl.ds(step * n, step)
        copies.append(pltpu.make_async_copy(y_hbm.at[rows], y_ref.at[rows], sems.at[n]))
    for copy in copies:
        copy.start()
    copies[0].wait()
    total = jnp.zeros((width, width), jnp.float32)
    per = 8
    nt = (((1,), (1,)), ((), ()))
    for c in range(0, blocks, per):
        if c % step == 0:
            copies[1 + c // step].wait()
        plain = jnp.concatenate([y_ref[d] for d in range(c, c + per)], axis=1)
        masked = jnp.concatenate([y_ref[d] * mask_ref[d : d + 1, :] for d in range(c, c + per)], axis=1)
        a_hi, a_lo = split(masked)
        b_hi, b_lo = split(plain)
        for a, b in ((a_hi, b_hi), (a_hi, b_lo), (a_lo, b_hi)):
            total = total + lax.dot_general(a, b, nt, preferred_element_type=jnp.float32)
    out_ref[:width, :] = total
    out_ref[width:, :] = jnp.full((8, width), counts_ref[0].astype(jnp.float32))


def unpack_kernel(in_ref, out_hbm, keep_ref, sems):
    chips = in_ref.shape[0]
    pieces = sems.shape[0]
    copies = []
    for n in range(pieces):
        for t in range(chips // pieces * n, chips // pieces * (n + 1)):
            keep_ref[:, LANES * t : LANES * (t + 1)] = in_ref[t]
        cols = pl.ds(LANES * (chips // pieces) * n, LANES * (chips // pieces))
        copies.append(pltpu.make_async_copy(keep_ref.at[:, cols], out_hbm.at[:, cols], sems.at[n]))
        copies[-1].start()
    for copy in copies:
        copy.wait()


def send(x, move):
    wide, high, core = (lax.axis_size(axis) for axis in AXES)
    pairs = []
    for w in range(wide):
        for h in range(high):
            for c in range(core):
                to = move(w, h, c)
                if to is not None:
                    pairs.append(((w * high + h) * core + c, (to[0] * high + to[1]) * core + to[2]))
    return lax.ppermute(x, AXES, pairs)


def paired_counts(counts):
    got, side = counts, 0
    for far_w, far_h in FAR:
        got = send(got, lambda w, h, c: (w ^ far_w, h ^ far_h, c) if c else None)
        side ^= far_w
    first = jnp.bitwise_and(lax.axis_index("wide"), side & -side) == 0
    return jnp.where(lax.axis_index("core") == 0, counts, jnp.where(first, counts + got, 0)), got


def half_sum(x):
    x = x + send(x, lambda w, h, c: (w, h, c ^ 1))
    x = x + sum(send(x, lambda w, h, c, n=n: (w, h ^ n, c)) for n in (1, 2, 3))
    x = x + sum(send(x, lambda w, h, c, n=n: (w ^ (n & 1), h ^ (2 * (n & 2)), c)) for n in (1, 2, 3))
    half = lax.axis_size("wide") // 4
    own = jnp.where(lax.axis_index("core") == 0, x, 0.0)
    for step in range(half):
        own = own + send(
            x,
            lambda w, h, c, step=step: (w ^ (2 * (step + half * c)), h, c) if step + c else None,
        )
    return own


def shards(panel, signs, sample_rows, counts):
    width, length = panel.shape
    slab = LOW * HIGH
    chips = lax.axis_size("wide") * lax.axis_size("high")
    samples = sample_rows.shape[0]
    scale = 1.0 / math.sqrt(slab * chips * lax.axis_size("core"))
    f32 = jnp.float32
    message = width + 1

    swap = [(0, 1), (1, 0)]
    other = lax.ppermute(panel, "core", swap)
    other_signs = lax.ppermute(signs, "core", swap)

    inputs = (sample_rows.reshape(1, samples), panel, signs.reshape(1, length))
    live, own = pl.pallas_call(
        prepare_kernel,
        in_specs=[SMEM] + [HBM] * 3,
        out_specs=(VMEM, VMEM),
        out_shape=(jax.ShapeDtypeStruct((chips, LANES), f32), jax.ShapeDtypeStruct((width, length), f32)),
        scratch_shapes=[
            pltpu.VMEM((1, samples), jnp.int32),
            pltpu.VMEM((width, length), f32),
            pltpu.VMEM((1, length), jnp.int32),
            pltpu.SemaphoreType.DMA((width // 8 + 2,)),
        ],
        compiler_params=PARAMS,
    )(counts, *(pltpu.with_memory_space_constraint(x, pltpu.HBM) for x in inputs))

    after, own = lax.optimization_barrier((counts, own))
    brought, step = paired_counts(after)

    sent = pl.pallas_call(
        lambda *refs: local_kernel(scale, *refs),
        out_shape=jax.ShapeDtypeStruct((message * chips, LANES), f32),
        scratch_shapes=[pltpu.VMEM((2, width * LOW, LANES), f32)],
        compiler_params=PARAMS,
    )(own, other, other_signs.reshape(1, length), live)

    sent, step = lax.optimization_barrier((sent, step))
    got = lax.all_to_all(sent.reshape(message * chips, 1, LANES), CHIP, 0, 0, tiled=True)

    mixed, mask = pl.pallas_call(
        lambda *refs: across_kernel(chips, width, *refs),
        in_specs=[VMEM],
        out_specs=(HBM, HBM),
        out_shape=(pltpu.HBM((chips, width, LANES), f32), pltpu.HBM((chips, LANES), f32)),
        scratch_shapes=[
            pltpu.VMEM((width * chips, LANES), f32),
            pltpu.VMEM((chips, LANES), f32),
            pltpu.SemaphoreType.DMA((width // 8 + 1,)),
        ],
        compiler_params=PARAMS,
    )(got.reshape(message * chips, LANES))

    back = lax.all_to_all(mixed, CHIP, 0, 0, tiled=True)

    part = pl.pallas_call(
        gram_kernel,
        in_specs=[SMEM, HBM, HBM],
        out_specs=VMEM,
        out_shape=jax.ShapeDtypeStruct((width + 8, width), f32),
        scratch_shapes=[
            pltpu.VMEM((chips, width, LANES), f32),
            pltpu.VMEM((chips, LANES), f32),
            pltpu.SemaphoreType.DMA((9,)),
        ],
        compiler_params=PARAMS,
    )(brought, *(pltpu.with_memory_space_constraint(x, pltpu.HBM) for x in (mixed, mask)))
    total = half_sum(part)
    total = total + send(total, lambda w, h, c: (w, h, c ^ 1))
    gram = total[:width] / total[width : width + 1]

    out = pl.pallas_call(
        unpack_kernel,
        in_specs=[VMEM],
        out_specs=HBM,
        out_shape=pltpu.HBM((width, length), f32),
        scratch_shapes=[pltpu.VMEM((width, length), f32), pltpu.SemaphoreType.DMA((8,))],
        compiler_params=PARAMS,
    )(back)
    return out, gram


def solution(mesh):
    wide, narrow = mesh.devices.shape
    mesh = Mesh(mesh.devices.reshape(wide, narrow // 2, 2), AXES)
    placed = (P(None, AXES), P(AXES), P(AXES), P(AXES))
    return jax.shard_map(
        shards,
        mesh=mesh,
        in_specs=placed,
        out_specs=(P(None, AXES), P()),
        check_vma=False,
    )
```
